128 devices in a mesh: dp: 4 (over z), lat: 16 (over y, x_lo, core), lon: 2 (over x_hi).
Axes of the slice: x: 4 (x_hi: 2, x_lo: 2; x = x_hi * 2 + x_lo), y: 4, z: 4, core: 2. Of those that a mesh axis runs over, the one named last changes fastest.
Arguments:
- fields: bfloat16 [4, 384, 768, 384], P('dp', 'lat', 'lon'), may hold values from -6 to 6
- cotangent: bfloat16 [4, 384, 768, 384], P('dp', 'lat', 'lon'), may hold values from -6 to 6
- w_first: bfloat16 [4, 2, 96, 96], P('lon'), may hold values from -0.4375 to 0.4375
- w_second: bfloat16 [4, 2, 96, 96], P('lon'), may hold values from -0.4375 to 0.4375
- bias_first: float32 [4, 2, 96], P('lon'), may hold values from -3 to 3
Outputs:
- grad_fields: bfloat16 [4, 384, 768, 384], P('dp', 'lat', 'lon')
- grad_w_first: float32 [4, 2, 96, 96], P('lon')
- grad_w_second: float32 [4, 2, 96, 96], P('lon')
- grad_bias_first: float32 [4, 2, 96], P('lon')
The draws below stay inside these ranges and needn't reach their ends.
All inputs are finite; a program needn't handle non-finite values.
Results may differ from the reference program's by a relative error of at most 0.012.
The reference program's roundings to bfloat16 on the way count: a program that leaves them out, or rounds other values in their place, can miss the bound.
Values may be sent and summed in bfloat16 or wider, within the bound.
A program may use at most 128 MiB of HBM per device.

```python
import math
import jax
import jax.numpy as jnp
from jax import lax

NLAT = 384
NLON = 768
KW = 96
BS = 96
NBLK = 4
CH = 384
BATCH = 4
SPEC_ROWS = 147456


def block_levels(stream_key, extent, shards, low, largest):
    level, own = 1.0, jax.random.fold_in(stream_key, 6)
    for dim, blocks in shards:
        steps = jnp.exp(jax.random.uniform(jax.random.fold_in(own, dim), (blocks,), jnp.float32, low / len(shards), largest / len(shards)))
        level = level * jnp.repeat(steps, extent[dim] // blocks).reshape([-1 if axis == dim else 1 for axis in range(len(extent))])
    return level


def bell_draw(rng, shape, deviation, most, shards=(), kind=jnp.bfloat16):
    level = block_levels(rng, shape, shards, -0.22, 0.18) if shards else 1.0
    result = jax.random.normal(rng, shape, jnp.float32) * deviation * level
    return jnp.minimum(jnp.maximum(result, -most), most).astype(kind)


def setup_inputs(seed: int = 0) -> dict:
    keys = jax.random.split(jax.random.key(seed), 6)
    fields = bell_draw(keys[0], (BATCH, NLAT, NLON, CH), 1.0, 6.0, ((0, 4), (1, 16), (2, 2)))
    cotangent = bell_draw(keys[1], (BATCH, NLAT, NLON, CH), 1.0, 6.0, ((0, 4), (1, 16), (2, 2)))
    w_first = bell_draw(keys[2], (NBLK, 2, BS, BS), (2 * BS) ** -0.5, 0.4375, ((0, 2),))
    w_second = bell_draw(keys[3], (NBLK, 2, BS, BS), (2 * BS) ** -0.5, 0.4375, ((0, 2),))
    bias_first = bell_draw(keys[4], (NBLK, 2, BS), 0.5, 3.0, ((0, 2),), jnp.float32)
    return dict(fields=fields, cotangent=cotangent, w_first=w_first, w_second=w_second, bias_first=bias_first)


shrink_level = 0.05
gelu_coef = 0.044715

def smooth_act(value):
    inner = math.sqrt(2.0 / math.pi) * (value + gelu_coef * value * value * value)
    return 0.5 * value * (1.0 + jnp.tanh(inner))

def smooth_slope(value):
    root = math.sqrt(2.0 / math.pi)
    tangent = jnp.tanh(root * (value + gelu_coef * value * value * value))
    return 0.5 * (1.0 + tangent) + 0.5 * value * (1.0 - tangent * tangent) * root * (1.0 + 3.0 * gelu_coef * value * value)

def shrink_gate(value):
    square = value * value
    return square / (square + shrink_level * shrink_level)

def lon_table(wavenums, longitudes):
    kk = jnp.arange(wavenums, dtype=jnp.int32)[:, None]
    ww = jnp.arange(longitudes, dtype=jnp.int32)[None, :]
    phase = (kk * ww % longitudes).astype(jnp.float32) * (2.0 * math.pi / longitudes)
    return jnp.stack([jnp.cos(phase), -jnp.sin(phase)], 0).astype(jnp.bfloat16)

def lat_table(latitudes):
    pp = jnp.arange(latitudes, dtype=jnp.int32)[:, None]
    hh = jnp.arange(latitudes, dtype=jnp.int32)[None, :]
    phase = (pp * hh % latitudes).astype(jnp.float32) * (2.0 * math.pi / latitudes)
    cosine = jnp.cos(phase)
    sine = jnp.sin(phase)
    return jnp.stack([jnp.stack([cosine, sine], 0), jnp.stack([-sine, cosine], 0)], 0).astype(jnp.bfloat16)

def complex_apply(zre, zim, weight):
    w_real = weight[:, 0].astype(jnp.float32)
    w_imag = weight[:, 1].astype(jnp.float32)
    zre = zre.astype(jnp.float32)
    zim = zim.astype(jnp.float32)
    real = jnp.einsum('nbi,bio->nbo', zre, w_real) - jnp.einsum('nbi,bio->nbo', zim, w_imag)
    imag = jnp.einsum('nbi,bio->nbo', zre, w_imag) + jnp.einsum('nbi,bio->nbo', zim, w_real)
    return (real, imag)

def complex_adjoint(dre, dim, weight):
    w_real = weight[:, 0].astype(jnp.float32)
    w_imag = weight[:, 1].astype(jnp.float32)
    dre = dre.astype(jnp.float32)
    dim = dim.astype(jnp.float32)
    real = jnp.einsum('nbo,bio->nbi', dre, w_real) + jnp.einsum('nbo,bio->nbi', dim, w_imag)
    imag = jnp.einsum('nbo,bio->nbi', dim, w_real) - jnp.einsum('nbo,bio->nbi', dre, w_imag)
    return (real, imag)

def complex_grad(zre, zim, dre, dim):
    zre = zre.astype(jnp.float32)
    zim = zim.astype(jnp.float32)
    dre = dre.astype(jnp.float32)
    dim = dim.astype(jnp.float32)
    real = jnp.einsum('nbi,nbo->bio', zre, dre) + jnp.einsum('nbi,nbo->bio', zim, dim)
    imag = jnp.einsum('nbi,nbo->bio', zre, dim) - jnp.einsum('nbi,nbo->bio', zim, dre)
    return jnp.stack([real, imag], 1)

def reference(fields, cotangent, w_first, w_second, bias_first):
    table_w = lon_table(KW, NLON).astype(jnp.float32)
    table_h = lat_table(NLAT).astype(jnp.float32)
    lon_norm = 1.0 / math.sqrt(NLON)
    lat_norm = 1.0 / math.sqrt(NLAT)
    doubling = jnp.where(jnp.arange(KW) == 0, 1.0, 2.0).astype(jnp.float32)[None, :, None]

    def one_sample(pair):
        field, cot = pair
        spec_a = (jnp.einsum('rkw,hwc->hrkc', table_w, field.astype(jnp.float32)) * lon_norm).astype(jnp.bfloat16)
        spec_g = (jnp.einsum('rkw,hwc->hrkc', table_w, cot.astype(jnp.float32)) * lon_norm).astype(jnp.bfloat16)
        freq = (jnp.einsum('qrph,hrkc->qpkc', table_h, spec_a.astype(jnp.float32)) * lat_norm).astype(jnp.bfloat16)
        gfreq = jnp.einsum('qrph,hrkc->qpkc', table_h, spec_g.astype(jnp.float32)) * lat_norm
        freq_re = freq[0].reshape(-1, NBLK, BS)
        freq_im = freq[1].reshape(-1, NBLK, BS)
        o1re, o1im = complex_apply(freq_re, freq_im, w_first)
        o1re = o1re + bias_first[:, 0]
        o1im = o1im + bias_first[:, 1]
        h1re = smooth_act(o1re).astype(jnp.bfloat16)
        h1im = smooth_act(o1im).astype(jnp.bfloat16)
        o2re, o2im = complex_apply(h1re, h1im, w_second)
        dre = (shrink_gate(o2re) * (gfreq[0] * doubling).reshape(-1, NBLK, BS)).astype(jnp.bfloat16)
        dim = (shrink_gate(o2im) * (gfreq[1] * doubling).reshape(-1, NBLK, BS)).astype(jnp.bfloat16)
        dhre, dhim = complex_adjoint(dre, dim, w_second)
        dzre = (smooth_slope(o1re) * dhre).astype(jnp.bfloat16)
        dzim = (smooth_slope(o1im) * dhim).astype(jnp.bfloat16)
        grad_two = complex_grad(h1re, h1im, dre, dim)
        grad_one = complex_grad(freq_re, freq_im, dzre, dzim)
        grad_bias = jnp.stack([lax.optimization_barrier(jnp.sum(dzre.astype(jnp.float32), 0)), lax.optimization_barrier(jnp.sum(dzim.astype(jnp.float32), 0))], 1)
        dsre, dsim = complex_adjoint(dzre, dzim, w_first)
        dspec = jnp.stack([dsre.reshape(NLAT, KW, CH), dsim.reshape(NLAT, KW, CH)], 0).astype(jnp.bfloat16)
        back = (jnp.einsum('qrph,qpkc->hrkc', table_h, dspec.astype(jnp.float32)) * lat_norm).astype(jnp.bfloat16)
        spatial = jnp.einsum('rkw,hrkc->hwc', table_w, back.astype(jnp.float32)) * lon_norm
        grad_field = (cot.astype(jnp.float32) + spatial).astype(jnp.bfloat16)
        return (grad_field, grad_one, grad_two, grad_bias)
    grad_fields, grads_one, grads_two, grads_bias = lax.map(one_sample, (fields, cotangent))
    scale = 1.0 / math.sqrt(SPEC_ROWS)
    return (grad_fields, lax.optimization_barrier(jnp.sum(grads_one, 0)) * scale, lax.optimization_barrier(jnp.sum(grads_two, 0)) * scale, lax.optimization_barrier(jnp.sum(grads_bias, 0)) * scale)
```

```python
import functools
import math

import jax
import jax.numpy as jnp
import numpy as np
from jax import lax
from jax.experimental import pallas as pl
from jax.experimental.pallas import tpu as pltpu
from jax.sharding import PartitionSpec as P

NLAT, NLON, KW, CH, BS, NBLK = 384, 768, 96, 384, 96, 4
HALF = NLON // 2
ROWS = 24
NG, GH = 3, 8
NJ = 3
ND = 8
NY = 4
SUB = 2 * GH
BLK = NG * SUB
QROWS = 4 * BLK
SPEC_ROWS = 4 * NLAT * KW

LON_NORM = 1.0 / math.sqrt(NLON)
LAT_NORM = 1.0 / math.sqrt(NLAT)
shrink_level = 0.05
gelu_coef = 0.044715
root = math.sqrt(2.0 / math.pi)

MESH = pl.DeviceIdType.MESH
F32, BF16 = jnp.float32, jnp.bfloat16


def cos_sin(phase_int, period):
    phase = phase_int.astype(np.float32) * np.float32(2.0 * math.pi / period)
    return np.cos(phase).astype(np.float32), np.sin(phase).astype(np.float32)


def tables():
    kk = np.arange(KW, dtype=np.int64)[:, None]
    ww = np.arange(NLON, dtype=np.int64)[None, :]
    cosine, sine = cos_sin(kk * ww % NLON, NLON)
    tw = np.stack([cosine, -sine], 1).reshape(2 * KW, 2, HALF).transpose(1, 0, 2)
    pp = np.arange(NLAT, dtype=np.int64)[:, None]
    hh = np.arange(NLAT, dtype=np.int64)[None, :]
    cosine, sine = cos_sin(pp * hh % NLAT, NLAT)
    th = np.stack([np.stack([cosine, sine], 0), np.stack([-sine, cosine], 0)], 0)
    th = th.transpose(0, 2, 1, 3).reshape(2 * NLAT, 2, NLAT // ROWS, NG, GH)
    th = th.transpose(0, 2, 3, 1, 4).reshape(2 * NLAT, 2 * NLAT)
    kind = jnp.bfloat16
    return (
        tw.astype(kind),
        np.ascontiguousarray(tw.transpose(0, 2, 1)).astype(kind),
        th.astype(kind),
        np.ascontiguousarray(th.T).astype(kind),
    )


def dot(a, b):
    return jnp.dot(a, b, preferred_element_type=F32)


def dot_nt(a, b):
    return lax.dot_general(a, b, (((1,), (1,)), ((), ())), preferred_element_type=F32)


def dot_tn(a, b):
    return lax.dot_general(a, b, (((0,), (0,)), ((), ())), preferred_element_type=F32)


def spectral_kernel(
    f_hbm,
    c_hbm,
    tw_ref,
    th_ref,
    tht_ref,
    wc1_ref,
    wc2_ref,
    bias_ref,
    back_hbm,
    g1_ref,
    g2_ref,
    gb_ref,
    fbuf,
    cbuf,
    ps,
    xs_f,
    xs_g,
    xr_f,
    xr_g,
    ys,
    yr,
    yb,
    yrb,
    zbuf,
    hbuf,
    dobuf,
    dzbuf,
    gmbuf,
    dsbuf,
    ld_sem,
    xl_sem,
    xsend,
    xrecv,
    yl_sem,
    ysend,
    yrecv,
):
    lat = lax.axis_index("lat")
    xhi = lax.axis_index("lon")
    dp = lax.axis_index("dp")
    y = lat // 4
    me = xhi * 4 + lax.rem(lat, 4)

    def device(yy, d):
        return (dp, yy * 4 + lax.rem(d, 4), d // 4)

    def load(which, g):
        src, dst = ((f_hbm, fbuf), (c_hbm, cbuf))[which]
        rows = pl.ds(g * GH, GH)
        return pltpu.make_async_copy(src.at[0, rows], dst.at[rows], ld_sem.at[which, g])

    for which in range(2):
        for g in range(NG):
            load(which, g).start()

    barrier = pltpu.get_barrier_semaphore()
    for i in range(1, ND):
        d = lax.rem(me + i, ND)
        pl.semaphore_signal(barrier, inc=1, device_id=device(y, d), device_id_type=MESH)
    for i in range(1, NY):
        yy = lax.rem(y + i, NY)
        pl.semaphore_signal(barrier, inc=1, device_id=device(yy, me), device_id_type=MESH)
    pl.semaphore_wait(barrier, ND - 1 + NY - 1)

    def x_refs(slot, d, frm):
        kind, i = slot // 3, slot % 3
        if kind == 0:
            return xs_f.at[i, d], xr_f.at[i, frm]
        if kind == 1:
            return xs_g.at[i, d], xr_g.at[i, frm]
        return yrb.at[i, :, pl.ds(pl.multiple_of(lax.rem(d, 4) * BLK, BLK), BLK)], back_hbm.at[i, frm]

    def x_copy(slot, d, frm):
        src, dst = x_refs(slot, d, frm)
        return pltpu.make_async_remote_copy(
            src_ref=src,
            dst_ref=dst,
            send_sem=xsend.at[slot, d],
            recv_sem=xrecv.at[slot, frm],
            device_id=device(y, d),
            device_id_type=MESH,
        )

    def x_local(slot):
        src, dst = x_refs(slot, me, me)
        return pltpu.make_async_copy(src, dst, xl_sem.at[slot])

    def x_start(slot):
        @pl.loop(1, ND)
        def _(i):
            x_copy(slot, lax.rem(me + i, ND), me).start()

        x_local(slot).start()

    def x_wait_recv(slot):
        @pl.loop(1, ND)
        def _(i):
            frm = lax.rem(me + ND - i, ND)
            x_copy(slot, frm, frm).wait_recv()

        x_local(slot).wait()

    def x_wait_send(slot):
        @pl.loop(1, ND)
        def _(i):
            x_copy(slot, lax.rem(me + i, ND), me).wait_send()

    def y_refs(slot, yy, frm):
        kind, j = slot // 3, slot % 3
        if kind < 2:
            return ys.at[kind, j, yy], yr.at[kind, j, frm]
        return yb.at[j, yy], yrb.at[j, frm]

    def y_copy(slot, yy, frm):
        src, dst = y_refs(slot, yy, frm)
        return pltpu.make_async_remote_copy(
            src_ref=src,
            dst_ref=dst,
            send_sem=ysend.at[slot, yy],
            recv_sem=yrecv.at[slot, frm],
            device_id=device(yy, me),
            device_id_type=MESH,
        )

    def y_local(slot):
        src, dst = y_refs(slot, y, y)
        return pltpu.make_async_copy(src, dst, yl_sem.at[slot])

    def y_start(slot):
        @pl.loop(1, NY)
        def _(i):
            y_copy(slot, lax.rem(y + i, NY), y).start()

        y_local(slot).start()

    def y_wait_recv(slot):
        @pl.loop(1, NY)
        def _(i):
            frm = lax.rem(y + NY - i, NY)
            y_copy(slot, frm, frm).wait_recv()

        y_local(slot).wait()

    def y_wait_send(slot):
        @pl.loop(1, NY)
        def _(i):
            y_copy(slot, lax.rem(y + i, NY), y).wait_send()

    def lon_group(which, g):
        buf = (fbuf, cbuf)[which]

        @pl.loop(0, GH)
        def _(h):
            part = dot(tw_ref[xhi], buf[g * GH + h])
            for ct in range(3):
                ps[ct, pl.ds(pl.multiple_of(h * 2 * KW, 2 * KW), 2 * KW), :] = part[
                    :, ct * 128 : (ct + 1) * 128
                ]

        @pl.loop(0, NJ * ND)
        def _(jd):
            j, d = jd // ND, lax.rem(jd, ND)
            for ky in range(NY):
                base = jd * (2 * NY) + 2 * ky
                for ct in range(3):
                    cols = pl.ds(ct * 128, 128)
                    tile = jnp.concatenate(
                        [ps[ct, pl.ds(base + r, GH, stride=2 * KW), :] for r in range(2)], 0
                    )
                    tile = (tile * LON_NORM).astype(BF16)
                    if which == 0:
                        xs_f[g, d, j * NY + ky, :, cols] = tile
                    else:
                        xs_g[j, d, ky, pl.ds(g * SUB, SUB), cols] = tile

    def x_sum_fields(j):
        @pl.loop(0, 4)
        def _(s):
            for ky in range(NY):
                for g in range(NG):
                    both = xr_f[g, s, j * NY + ky].astype(F32) + xr_f[g, s + 4, j * NY + ky].astype(
                        F32
                    )
                    rows = pl.ds(pl.multiple_of(s * BLK + g * SUB, SUB), SUB)
                    ys[0, j, ky, rows, :] = both.astype(BF16)

    def x_sum_cot(j):
        @pl.loop(0, 4)
        def _(s):
            for ky in range(NY):
                both = xr_g[j, s, ky].astype(F32) + xr_g[j, s + 4, ky].astype(F32)
                rows = pl.ds(pl.multiple_of(s * BLK, BLK), BLK)
                ys[1, j, ky, rows, :] = both.astype(BF16)

    TILE = 192

    def spectral(j):
        wave = (j * ND + me) * NY + y
        doubling = jnp.where(wave == 0, 1.0, 2.0).astype(F32) * LAT_NORM

        @pl.loop(0, 2)
        def _(t):
            rows = pl.ds(pl.multiple_of(t * TILE, TILE), TILE)
            for q in range(2):
                trows = pl.ds(pl.multiple_of(q * NLAT + t * TILE, TILE), TILE)
                cols = pl.ds(q * CH, CH)
                left = th_ref[trows, :]
                zbuf[rows, cols] = (
                    dot(left, yr[0, j].reshape(2 * NLAT, CH)) * LAT_NORM
                ).astype(BF16)
                gmbuf[rows, cols] = dot(left, yr[1, j].reshape(2 * NLAT, CH)) * doubling

        @pl.loop(0, 2)
        def _(t):
            rows = pl.ds(pl.multiple_of(t * TILE, TILE), TILE)
            o1 = dot(zbuf[rows, :], wc1_ref[...]) + bias_ref[...]
            square = o1 * o1
            tangent = jnp.tanh(root * (o1 + gelu_coef * o1 * square))
            hbuf[rows, :] = (0.5 * o1 * (1.0 + tangent)).astype(BF16)
            slope = 0.5 * (1.0 + tangent) + 0.5 * o1 * (1.0 - tangent * tangent) * root * (
                1.0 + 3.0 * gelu_coef * square
            )
            o2 = dot(hbuf[rows, :], wc2_ref[...])
            square = o2 * o2
            keep = square / (square + shrink_level * shrink_level)
            dobuf[rows, :] = (keep * gmbuf[rows, :]).astype(BF16)
            dh = dot_nt(dobuf[rows, :], wc2_ref[...])
            dz = (slope * dh).astype(BF16)
            dzbuf[rows, :] = dz
            gb_ref[...] += jnp.sum(dz.astype(F32), 0, keepdims=True)
            ds = dot_nt(dz, wc1_ref[...]).astype(BF16)
            for q in range(2):
                trows = pl.ds(pl.multiple_of(q * NLAT + t * TILE, TILE), TILE)
                dsbuf[trows, :] = ds[:, q * CH : (q + 1) * CH]

        @pl.loop(0, NY)
        def _(yy):
            rows = pl.ds(pl.multiple_of(yy * QROWS, QROWS), QROWS)
            yb[j, yy] = (dot(tht_ref[rows, :], dsbuf[...]) * LAT_NORM).astype(BF16)

        y_start(6 + j)

        re, im = pl.ds(0, CH), pl.ds(CH, CH)
        for zz, dd, out in ((zbuf, dzbuf, g1_ref), (hbuf, dobuf, g2_ref)):
            out[0] += dot_tn(zz[:, re], dd[:, re]) + dot_tn(zz[:, im], dd[:, im])
            out[1] += dot_tn(zz[:, re], dd[:, im]) - dot_tn(zz[:, im], dd[:, re])

    g1_ref[...] = jnp.zeros_like(g1_ref)
    g2_ref[...] = jnp.zeros_like(g2_ref)
    gb_ref[...] = jnp.zeros_like(gb_ref)

    for g in range(NG):
        load(0, g).wait()
        lon_group(0, g)
        x_start(g)
    for g in range(NG):
        load(1, g).wait()
        lon_group(1, g)
    x_wait_recv(0)
    x_wait_recv(1)
    x_start(3)
    x_wait_recv(2)
    x_start(4)
    for j in range(NJ):
        x_sum_fields(j)
        y_start(j)

    x_wait_recv(3)
    x_start(5)
    x_sum_cot(0)
    y_start(3)
    for j in range(NJ):
        y_wait_recv(j)
    y_wait_recv(3)
    spectral(0)
    x_wait_recv(4)
    x_sum_cot(1)
    y_start(4)
    y_wait_recv(6)
    x_start(6)
    y_wait_recv(4)
    spectral(1)
    x_wait_recv(5)
    x_sum_cot(2)
    y_start(5)
    y_wait_recv(7)
    x_start(7)
    y_wait_recv(5)
    spectral(2)
    y_wait_recv(8)
    x_start(8)
    for slot in range(9):
        if slot >= 6:
            x_wait_recv(slot)
        x_wait_send(slot)
        y_wait_send(slot)


def spectral_call(fields, cotangent, tw, th, tht, wc1, wc2, bias):
    vm = pl.BlockSpec(memory_space=pltpu.VMEM)
    hbm = pl.BlockSpec(memory_space=pl.ANY)
    dma = pltpu.SemaphoreType.DMA
    return pl.pallas_call(
        spectral_kernel,
        out_shape=(
            jax.ShapeDtypeStruct((NJ, ND, NY, BLK, CH), BF16),
            jax.ShapeDtypeStruct((2, CH, CH), F32),
            jax.ShapeDtypeStruct((2, CH, CH), F32),
            jax.ShapeDtypeStruct((1, 2 * CH), F32),
        ),
        in_specs=[hbm, hbm] + [vm] * 6,
        out_specs=(hbm, vm, vm, vm),
        scratch_shapes=[
            pltpu.VMEM((ROWS, HALF, CH), BF16),
            pltpu.VMEM((ROWS, HALF, CH), BF16),
            pltpu.VMEM((3, GH * 2 * KW, 128), F32),
            pltpu.VMEM((NG, ND, NJ * NY, SUB, CH), BF16),
            pltpu.VMEM((NJ, ND, NY, BLK, CH), BF16),
            pltpu.VMEM((NG, ND, NJ * NY, SUB, CH), BF16),
            pltpu.VMEM((NJ, ND, NY, BLK, CH), BF16),
            pltpu.VMEM((2, NJ, NY, QROWS, CH), BF16),
            pltpu.VMEM((2, NJ, NY, QROWS, CH), BF16),
            pltpu.VMEM((NJ, NY, QROWS, CH), BF16),
            pltpu.VMEM((NJ, NY, QROWS, CH), BF16),
            pltpu.VMEM((NLAT, 2 * CH), BF16),
            pltpu.VMEM((NLAT, 2 * CH), BF16),
            pltpu.VMEM((NLAT, 2 * CH), BF16),
            pltpu.VMEM((NLAT, 2 * CH), BF16),
            pltpu.VMEM((NLAT, 2 * CH), F32),
            pltpu.VMEM((2 * NLAT, CH), BF16),
            dma((2, NG)),
            dma((9,)),
            dma((9, ND)),
            dma((9, ND)),
            dma((9,)),
            dma((9, NY)),
            dma((9, NY)),
        ],
        compiler_params=pltpu.CompilerParams(
            collective_id=0, has_side_effects=True, vmem_limit_bytes=62 << 20
        ),
        cost_estimate=pl.CostEstimate(flops=10**10, bytes_accessed=3 * 10**7, transcendentals=10**6),
        name="spectral",
    )(fields, cotangent, tw, th, tht, wc1, wc2, bias)


def inverse_kernel(back_ref, cot_ref, twt_ref, out_ref, bs):
    xhi = lax.axis_index("lon")

    @pl.loop(0, NJ * ND)
    def _(jd):
        j, d = jd // ND, lax.rem(jd, ND)
        for ky in range(NY):
            rows = pl.ds(pl.multiple_of(jd * NY * SUB + ky * SUB, SUB), SUB)
            for ct in range(3):
                bs[ct, rows, :] = back_ref[j, d, ky, :, pl.ds(ct * 128, 128)].astype(F32)

    @pl.loop(0, GH)
    def _(h):
        spec = jnp.concatenate(
            [bs[ct, pl.ds(h, 2 * KW, stride=GH), :].astype(BF16) for ct in range(3)], 1
        )
        spatial = dot(twt_ref[xhi], spec) * LON_NORM
        out_ref[0, h] = (cot_ref[0, h].astype(F32) + spatial).astype(BF16)


def inverse_call(back, cotangent, twt):
    return pl.pallas_call(
        inverse_kernel,
        grid=(NG,),
        out_shape=jax.ShapeDtypeStruct((1, ROWS, HALF, CH), BF16),
        in_specs=[
            pl.BlockSpec((NJ, ND, NY, SUB, CH), lambda g: (0, 0, 0, g, 0)),
            pl.BlockSpec((1, GH, HALF, CH), lambda g: (0, g, 0, 0)),
            pl.BlockSpec((2, HALF, 2 * KW), lambda g: (0, 0, 0)),
        ],
        out_specs=pl.BlockSpec((1, GH, HALF, CH), lambda g: (0, g, 0, 0)),
        scratch_shapes=[pltpu.VMEM((3, GH * 2 * KW, 128), F32)],
        compiler_params=pltpu.CompilerParams(vmem_limit_bytes=48 << 20),
        cost_estimate=pl.CostEstimate(
            flops=1400 * 10**6, bytes_accessed=18 * 10**6, transcendentals=0
        ),
        name="inverse",
    )(back, cotangent, twt)


def dense_weight(weight):
    parts = [jax.scipy.linalg.block_diag(*[weight[n, r] for n in range(NBLK)]) for r in range(2)]
    return jnp.concatenate(
        [
            jnp.concatenate([parts[0], parts[1]], 1),
            jnp.concatenate([-parts[1], parts[0]], 1),
        ],
        0,
    )


def both_halves(mine):
    other = lax.ppermute(mine, "lon", [(0, 1), (1, 0)])
    first = lax.axis_index("lon") == 0
    return jnp.concatenate([jnp.where(first, mine, other), jnp.where(first, other, mine)], 0)


def on_device(fields, cotangent, w_first, w_second, bias_first):
    tw, twt, th, tht = tables()
    weights = both_halves(jnp.stack([w_first, w_second], 1))
    bias = both_halves(bias_first).transpose(1, 0, 2).reshape(1, 2 * CH)
    wc1, wc2 = dense_weight(weights[:, 0]), dense_weight(weights[:, 1])
    back, grad_one, grad_two, grad_bias = spectral_call(
        fields, cotangent, jnp.asarray(tw), jnp.asarray(th), jnp.asarray(tht), wc1, wc2, bias
    )
    grad_fields = inverse_call(back, cotangent, jnp.asarray(twt))

    def blocks(grad):
        return jnp.stack([grad[:, n * BS : (n + 1) * BS, n * BS : (n + 1) * BS] for n in range(NBLK)])

    grads = (blocks(grad_one), blocks(grad_two), grad_bias.reshape(2, NBLK, BS).transpose(1, 0, 2))
    grads = lax.psum(grads, ("dp", "lat", "lon"))
    scale = 1.0 / math.sqrt(SPEC_ROWS)
    here = lax.axis_index("lon") * 2
    grads = [lax.dynamic_slice_in_dim(grad * scale, here, 2, 0) for grad in grads]
    return (grad_fields, *grads)


def solution(mesh):
    placed = (
        P("dp", "lat", "lon", None),
        P("dp", "lat", "lon", None),
        P("lon", None, None, None),
        P("lon", None, None, None),
        P("lon", None, None),
    )
    return jax.shard_map(
        on_device,
        mesh=mesh,
        in_specs=placed,
        out_specs=(
            P("dp", "lat", "lon", None),
            P("lon", None, None, None),
            P("lon", None, None, None),
            P("lon", None, None),
        ),
        check_vma=False,
    )
```

```python
import functools
import math

import jax
import jax.numpy as jnp
import numpy as np
from jax import lax
from jax.experimental import pallas as pl
from jax.experimental.pallas import tpu as pltpu
from jax.sharding import PartitionSpec as P

NLAT, NLON, KW, CH, BS, NBLK = 384, 768, 96, 384, 96, 4
HALF = NLON // 2
ROWS = 24
NG, GH = 3, 8
NJ = 3
ND = 8
NY = 4
NZ = 4
SUB = 2 * GH
BLK = NG * SUB
QROWS = 4 * BLK
SPEC_ROWS = 4 * NLAT * KW

LON_NORM = 1.0 / math.sqrt(NLON)
LAT_NORM = 1.0 / math.sqrt(NLAT)
shrink_level = 0.05
gelu_coef = 0.044715
root = math.sqrt(2.0 / math.pi)

MESH = pl.DeviceIdType.MESH
F32, BF16 = jnp.float32, jnp.bfloat16


def cos_sin(phase_int, period):
    phase = phase_int.astype(np.float32) * np.float32(2.0 * math.pi / period)
    return np.cos(phase).astype(np.float32), np.sin(phase).astype(np.float32)


def tables():
    kk = np.arange(KW, dtype=np.int64)[:, None]
    ww = np.arange(NLON, dtype=np.int64)[None, :]
    cosine, sine = cos_sin(kk * ww % NLON, NLON)
    tw = np.stack([cosine, -sine], 1).reshape(2 * KW, 2, HALF).transpose(1, 0, 2)
    pp = np.arange(NLAT, dtype=np.int64)[:, None]
    hh = np.arange(NLAT, dtype=np.int64)[None, :]
    cosine, sine = cos_sin(pp * hh % NLAT, NLAT)
    th = np.stack([np.stack([cosine, sine], 0), np.stack([-sine, cosine], 0)], 0)
    th = th.transpose(0, 2, 1, 3).reshape(2 * NLAT, 2, NLAT // ROWS, NG, GH)
    th = th.transpose(0, 2, 3, 1, 4).reshape(2 * NLAT, 2 * NLAT)
    kind = jnp.bfloat16
    return (
        tw.astype(kind),
        np.ascontiguousarray(tw.transpose(0, 2, 1)).astype(kind),
        th.astype(kind),
        np.ascontiguousarray(th.T).astype(kind),
    )


def dot(a, b):
    return jnp.dot(a, b, preferred_element_type=F32)


def dot_nt(a, b):
    return lax.dot_general(a, b, (((1,), (1,)), ((), ())), preferred_element_type=F32)


def dot_tn(a, b):
    return lax.dot_general(a, b, (((0,), (0,)), ((), ())), preferred_element_type=F32)


def spectral_kernel(
    f_hbm,
    c_hbm,
    tw_ref,
    th_ref,
    tht_ref,
    w1_ref,
    w2_ref,
    b1_ref,
    back_hbm,
    gout_ref,
    gbout_ref,
    w_all,
    b_all,
    wc1_ref,
    wc2_ref,
    bias_ref,
    gacc,
    gb_ref,
    gz,
    gzr,
    gy,
    gyr,
    gd,
    gdr,
    gyo,
    gzo,
    fbuf,
    cbuf,
    ps,
    xs_f,
    xs_g,
    xr_f,
    xr_g,
    ys,
    yr,
    yb,
    yrb,
    zbuf,
    hbuf,
    dobuf,
    dzbuf,
    gmbuf,
    dsbuf,
    ld_sem,
    xl_sem,
    xsend,
    xrecv,
    yl_sem,
    ysend,
    yrecv,
    wl_sem,
    wsend,
    wrecv,
    gsend,
    grecv,
):
    lat = lax.axis_index("lat")
    xhi = lax.axis_index("lon")
    dp = lax.axis_index("dp")
    y = lat // 4
    me = xhi * 4 + lax.rem(lat, 4)

    def device(yy, d, zz=dp):
        return (zz, yy * 4 + lax.rem(d, 4), d // 4)

    def load(which, g):
        src, dst = ((f_hbm, fbuf), (c_hbm, cbuf))[which]
        rows = pl.ds(g * GH, GH)
        return pltpu.make_async_copy(src.at[0, rows], dst.at[rows], ld_sem.at[which, g])

    for which in range(2):
        for g in range(NG):
            load(which, g).start()

    barrier = pltpu.get_barrier_semaphore()
    for i in range(1, ND):
        d = lax.rem(me + i, ND)
        pl.semaphore_signal(barrier, inc=1, device_id=device(y, d), device_id_type=MESH)
    for i in range(1, NY):
        yy = lax.rem(y + i, NY)
        pl.semaphore_signal(barrier, inc=1, device_id=device(yy, me), device_id_type=MESH)
    for i in range(1, NZ):
        zz = lax.rem(dp + i, NZ)
        pl.semaphore_signal(barrier, inc=1, device_id=device(y, me, zz), device_id_type=MESH)
    pl.semaphore_wait(barrier, ND - 1 + NY - 1 + NZ - 1)

    def weight_refs(i):
        return ((w1_ref, w_all.at[0, xhi]), (w2_ref, w_all.at[1, xhi]), (b1_ref, b_all.at[xhi]))[i]

    def weight_copy(i):
        src, dst = weight_refs(i)
        return pltpu.make_async_remote_copy(
            src_ref=src,
            dst_ref=dst,
            send_sem=wsend.at[i],
            recv_sem=wrecv.at[i],
            device_id=device(y, lax.rem(me + 4, ND)),
            device_id_type=MESH,
        )

    def weight_local(i):
        src, dst = weight_refs(i)
        return pltpu.make_async_copy(src, dst, wl_sem.at[i])

    def weights_start():
        for i in range(3):
            weight_copy(i).start()
            weight_local(i).start()

    def weights_build():
        for i in range(3):
            weight_copy(i).wait()
            weight_local(i).wait()
        row = lax.broadcasted_iota(jnp.int32, (BS, CH), 0)
        col = lax.broadcasted_iota(jnp.int32, (BS, CH), 1)
        bias = jnp.zeros((2, CH), F32)
        for n in range(NBLK):
            spread = col == row + n * BS
            bias += jnp.dot(
                b_all[n // 2, n % 2],
                spread.astype(F32),
                precision=lax.Precision.HIGHEST,
                preferred_element_type=F32,
            )
            spread = spread.astype(F32).astype(BF16)
            top, low = pl.ds(n * BS, BS), pl.ds(CH + n * BS, BS)
            re, im = pl.ds(0, CH), pl.ds(CH, CH)
            for i, out in enumerate((wc1_ref, wc2_ref)):
                real = dot(w_all[i, n // 2, n % 2, 0], spread)
                imag = dot(w_all[i, n // 2, n % 2, 1], spread)
                out[top, re] = real.astype(BF16)
                out[low, im] = real.astype(BF16)
                out[top, im] = imag.astype(BF16)
                out[low, re] = (-imag).astype(BF16)
        for r in range(2):
            bias_ref[:, pl.ds(r * CH, CH)] = bias[r : r + 1]

    def x_refs(slot, d, frm):
        kind, i = slot // 3, slot % 3
        if kind == 0:
            return xs_f.at[i, d], xr_f.at[i, frm]
        if kind == 1:
            return xs_g.at[i, d], xr_g.at[i, frm]
        return yrb.at[i, :, pl.ds(pl.multiple_of(lax.rem(d, 4) * BLK, BLK), BLK)], back_hbm.at[i, frm]

    def x_copy(slot, d, frm):
        src, dst = x_refs(slot, d, frm)
        return pltpu.make_async_remote_copy(
            src_ref=src,
            dst_ref=dst,
            send_sem=xsend.at[slot, d],
            recv_sem=xrecv.at[slot, frm],
            device_id=device(y, d),
            device_id_type=MESH,
        )

    def x_local(slot):
        src, dst = x_refs(slot, me, me)
        return pltpu.make_async_copy(src, dst, xl_sem.at[slot])

    def x_start(slot):
        @pl.loop(1, ND)
        def _(i):
            x_copy(slot, lax.rem(me + i, ND), me).start()

        x_local(slot).start()

    def x_wait_recv(slot):
        @pl.loop(1, ND)
        def _(i):
            frm = lax.rem(me + ND - i, ND)
            x_copy(slot, frm, frm).wait_recv()

        x_local(slot).wait()

    def x_wait_send(slot):
        @pl.loop(1, ND)
        def _(i):
            x_copy(slot, lax.rem(me + i, ND), me).wait_send()

    def y_refs(slot, yy, frm):
        kind, j = slot // 3, slot % 3
        if kind < 2:
            return ys.at[kind, j, yy], yr.at[kind, j, frm]
        return yb.at[j, yy], yrb.at[j, frm]

    def y_copy(slot, yy, frm):
        src, dst = y_refs(slot, yy, frm)
        return pltpu.make_async_remote_copy(
            src_ref=src,
            dst_ref=dst,
            send_sem=ysend.at[slot, yy],
            recv_sem=yrecv.at[slot, frm],
            device_id=device(yy, me),
            device_id_type=MESH,
        )

    def y_local(slot):
        src, dst = y_refs(slot, y, y)
        return pltpu.make_async_copy(src, dst, yl_sem.at[slot])

    def y_start(slot):
        @pl.loop(1, NY)
        def _(i):
            y_copy(slot, lax.rem(y + i, NY), y).start()

        y_local(slot).start()

    def y_wait_recv(slot):
        @pl.loop(1, NY)
        def _(i):
            frm = lax.rem(y + NY - i, NY)
            y_copy(slot, frm, frm).wait_recv()

        y_local(slot).wait()

    def y_wait_send(slot):
        @pl.loop(1, NY)
        def _(i):
            y_copy(slot, lax.rem(y + i, NY), y).wait_send()

    def lon_group(which, g):
        buf = (fbuf, cbuf)[which]

        @pl.loop(0, GH)
        def _(h):
            part = dot(tw_ref[xhi], buf[g * GH + h])
            for ct in range(3):
                ps[ct, pl.ds(pl.multiple_of(h * 2 * KW, 2 * KW), 2 * KW), :] = part[
                    :, ct * 128 : (ct + 1) * 128
                ]

        @pl.loop(0, NJ * ND)
        def _(jd):
            j, d = jd // ND, lax.rem(jd, ND)
            for ky in range(NY):
                base = jd * (2 * NY) + 2 * ky
                for ct in range(3):
                    cols = pl.ds(ct * 128, 128)
                    tile = jnp.concatenate(
                        [ps[ct, pl.ds(base + r, GH, stride=2 * KW), :] for r in range(2)], 0
                    )
                    tile = (tile * LON_NORM).astype(BF16)
                    if which == 0:
                        xs_f[g, d, j * NY + ky, :, cols] = tile
                    else:
                        xs_g[j, d, ky, pl.ds(g * SUB, SUB), cols] = tile

    def x_sum_fields(j):
        @pl.loop(0, 4)
        def _(s):
            for ky in range(NY):
                for g in range(NG):
                    both = xr_f[g, s, j * NY + ky].astype(F32) + xr_f[g, s + 4, j * NY + ky].astype(
                        F32
                    )
                    rows = pl.ds(pl.multiple_of(s * BLK + g * SUB, SUB), SUB)
                    ys[0, j, ky, rows, :] = both.astype(BF16)

    def x_sum_cot(j):
        @pl.loop(0, 4)
        def _(s):
            for ky in range(NY):
                both = xr_g[j, s, ky].astype(F32) + xr_g[j, s + 4, ky].astype(F32)
                rows = pl.ds(pl.multiple_of(s * BLK, BLK), BLK)
                ys[1, j, ky, rows, :] = both.astype(BF16)

    TILE = 192

    def spectral(j):
        wave = (j * ND + me) * NY + y
        doubling = jnp.where(wave == 0, 1.0, 2.0).astype(F32) * LAT_NORM

        @pl.loop(0, 2)
        def _(t):
            rows = pl.ds(pl.multiple_of(t * TILE, TILE), TILE)
            for q in range(2):
                trows = pl.ds(pl.multiple_of(q * NLAT + t * TILE, TILE), TILE)
                cols = pl.ds(q * CH, CH)
                left = th_ref[trows, :]
                zbuf[rows, cols] = (
                    dot(left, yr[0, j].reshape(2 * NLAT, CH)) * LAT_NORM
                ).astype(BF16)
                gmbuf[rows, cols] = dot(left, yr[1, j].reshape(2 * NLAT, CH)) * doubling

        @pl.loop(0, 2)
        def _(t):
            rows = pl.ds(pl.multiple_of(t * TILE, TILE), TILE)
            o1 = dot(zbuf[rows, :], wc1_ref[...]) + bias_ref[...]
            square = o1 * o1
            tangent = jnp.tanh(root * (o1 + gelu_coef * o1 * square))
            hbuf[rows, :] = (0.5 * o1 * (1.0 + tangent)).astype(BF16)
            slope = 0.5 * (1.0 + tangent) + 0.5 * o1 * (1.0 - tangent * tangent) * root * (
                1.0 + 3.0 * gelu_coef * square
            )
            o2 = dot(hbuf[rows, :], wc2_ref[...])
            square = o2 * o2
            keep = square / (square + shrink_level * shrink_level)
            dobuf[rows, :] = (keep * gmbuf[rows, :]).astype(BF16)
            dh = dot_nt(dobuf[rows, :], wc2_ref[...])
            dz = (slope * dh).astype(BF16)
            dzbuf[rows, :] = dz
            gb_ref[...] += jnp.sum(dz.astype(F32), 0, keepdims=True)
            ds = dot_nt(dz, wc1_ref[...]).astype(BF16)
            for q in range(2):
                trows = pl.ds(pl.multiple_of(q * NLAT + t * TILE, TILE), TILE)
                dsbuf[trows, :] = ds[:, q * CH : (q + 1) * CH]

        @pl.loop(0, NY)
        def _(yy):
            rows = pl.ds(pl.multiple_of(yy * QROWS, QROWS), QROWS)
            yb[j, yy] = (dot(tht_ref[rows, :], dsbuf[...]) * LAT_NORM).astype(BF16)

        y_start(6 + j)

        re, im = pl.ds(0, CH), pl.ds(CH, CH)
        for i, (zz, dd) in enumerate(((zbuf, dzbuf), (hbuf, dobuf))):
            gacc[2 * i] += dot_tn(zz[:, re], dd[:, re]) + dot_tn(zz[:, im], dd[:, im])
            gacc[2 * i + 1] += dot_tn(zz[:, re], dd[:, im]) - dot_tn(zz[:, im], dd[:, re])

    def grad_copy(stage, to, frm):
        src, dst, target = (
            lambda: (gz.at[to], gzr.at[frm], device(y, me, to)),
            lambda: (gy.at[to], gyr.at[frm], device(to, me)),
            lambda: (gd, gdr.at[frm], device(y, to)),
            lambda: (gd.at[pl.ds(0, BS // NY)], gyo.at[frm], device(to, me)),
            lambda: (gyo, gzo.at[frm], device(y, me, to)),
        )[stage]()
        return pltpu.make_async_remote_copy(
            src_ref=src,
            dst_ref=dst,
            send_sem=gsend.at[stage, to],
            recv_sem=grecv.at[stage, frm],
            device_id=target,
            device_id_type=MESH,
        )

    stage_size = (NZ, NY, ND, NY, NZ)
    stage_place = (dp, y, me, y, dp)

    def grad_start(stage):
        here, size = stage_place[stage], stage_size[stage]

        @pl.loop(1, size)
        def _(i):
            grad_copy(stage, lax.rem(here + i, size), here).start()

    def grad_wait(stage):
        here, size = stage_place[stage], stage_size[stage]

        @pl.loop(1, size)
        def _(i):
            frm = lax.rem(here + size - i, size)
            grad_copy(stage, frm, frm).wait_recv()

        @pl.loop(1, size)
        def _(i):
            grad_copy(stage, lax.rem(here + i, size), here).wait_send()

    def grad_begin():
        lane = lax.broadcasted_iota(jnp.int32, (BS, CH), 1)
        line = lax.broadcasted_iota(jnp.int32, (8, CH), 0)
        both = [jnp.broadcast_to(gb_ref[:, pl.ds(r * CH, CH)], (8, CH)) for r in range(2)]
        sums = jnp.where(line == 0, both[0], jnp.where(line == 1, both[1], 0.0))
        for i in range(NZ):
            part = gacc[i, pl.ds(0, BS), :]
            for n in range(1, NBLK):
                part = jnp.where(lane >= n * BS, gacc[i, pl.ds(n * BS, BS), :], part)
            gz[i, pl.ds(0, BS), :] = part
            gz[i, pl.ds(BS, 8), :] = sums
        gzr[dp] = gz[dp]
        grad_start(0)

    def grad_finish():
        part = BS // NY
        grad_wait(0)
        total = gzr[0] + gzr[1] + gzr[2] + gzr[3]
        for i in range(NY):
            gy[i, pl.ds(0, part), :] = total[i * part : (i + 1) * part]
            gy[i, pl.ds(part, 8), :] = total[BS:]
        gyr[y] = gy[y]
        grad_start(1)
        grad_wait(1)
        gd[...] = gyr[0] + gyr[1] + gyr[2] + gyr[3]
        gdr[me] = gd[...]
        grad_start(2)
        grad_wait(2)
        total = gdr[0]
        for i in range(1, ND):
            total += gdr[i]
        gd[...] = total
        gbout_ref[...] = total[part:]
        gyo[y] = total[:part]
        grad_start(3)
        grad_wait(3)
        gzo[dp] = gyo[...]
        grad_start(4)
        grad_wait(4)
        gout_ref[...] = gzo[...]

    weights_start()
    gacc[...] = jnp.zeros_like(gacc)
    gb_ref[...] = jnp.zeros_like(gb_ref)

    for g in range(NG):
        load(0, g).wait()
        lon_group(0, g)
        x_start(g)
    for g in range(NG):
        load(1, g).wait()
        lon_group(1, g)
    weights_build()
    x_wait_recv(0)
    x_wait_recv(1)
    x_start(3)
    x_wait_recv(2)
    x_start(4)
    for j in range(NJ):
        x_sum_fields(j)
        y_start(j)

    x_wait_recv(3)
    x_start(5)
    x_sum_cot(0)
    y_start(3)
    for j in range(NJ):
        y_wait_recv(j)
    y_wait_recv(3)
    spectral(0)
    x_wait_recv(4)
    x_sum_cot(1)
    y_start(4)
    y_wait_recv(6)
    x_start(6)
    y_wait_recv(4)
    spectral(1)
    x_wait_recv(5)
    x_sum_cot(2)
    y_start(5)
    y_wait_recv(7)
    x_start(7)
    y_wait_recv(5)
    spectral(2)
    grad_begin()
    y_wait_recv(8)
    x_start(8)
    grad_finish()
    for slot in range(9):
        if slot >= 6:
            x_wait_recv(slot)
        x_wait_send(slot)
        y_wait_send(slot)


def spectral_call(fields, cotangent, tw, th, tht, w_first, w_second, bias):
    vm = pl.BlockSpec(memory_space=pltpu.VMEM)
    hbm = pl.BlockSpec(memory_space=pl.ANY)
    dma = pltpu.SemaphoreType.DMA
    return pl.pallas_call(
        spectral_kernel,
        out_shape=(
            jax.ShapeDtypeStruct((NJ, ND, NY, BLK, CH), BF16),
            jax.ShapeDtypeStruct((NZ, NY, BS // NY, CH), F32),
            jax.ShapeDtypeStruct((8, CH), F32),
        ),
        in_specs=[hbm, hbm] + [vm] * 6,
        out_specs=(hbm, vm, vm),
        scratch_shapes=[
            pltpu.VMEM((2, 2, 2, 2, BS, BS), BF16),
            pltpu.VMEM((2, 2, 2, BS), F32),
            pltpu.VMEM((2 * CH, 2 * CH), BF16),
            pltpu.VMEM((2 * CH, 2 * CH), BF16),
            pltpu.VMEM((1, 2 * CH), F32),
            pltpu.VMEM((4, CH, CH), F32),
            pltpu.VMEM((1, 2 * CH), F32),
            pltpu.VMEM((NZ, BS + 8, CH), F32),
            pltpu.VMEM((NZ, BS + 8, CH), F32),
            pltpu.VMEM((NY, BS // NY + 8, CH), F32),
            pltpu.VMEM((NY, BS // NY + 8, CH), F32),
            pltpu.VMEM((BS // NY + 8, CH), F32),
            pltpu.VMEM((ND, BS // NY + 8, CH), F32),
            pltpu.VMEM((NY, BS // NY, CH), F32),
            pltpu.VMEM((NZ, NY, BS // NY, CH), F32),
            pltpu.VMEM((ROWS, HALF, CH), BF16),
            pltpu.VMEM((ROWS, HALF, CH), BF16),
            pltpu.VMEM((3, GH * 2 * KW, 128), F32),
            pltpu.VMEM((NG, ND, NJ * NY, SUB, CH), BF16),
            pltpu.VMEM((NJ, ND, NY, BLK, CH), BF16),
            pltpu.VMEM((NG, ND, NJ * NY, SUB, CH), BF16),
            pltpu.VMEM((NJ, ND, NY, BLK, CH), BF16),
            pltpu.VMEM((2, NJ, NY, QROWS, CH), BF16),
            pltpu.VMEM((2, NJ, NY, QROWS, CH), BF16),
            pltpu.VMEM((NJ, NY, QROWS, CH), BF16),
            pltpu.VMEM((NJ, NY, QROWS, CH), BF16),
            pltpu.VMEM((NLAT, 2 * CH), BF16),
            pltpu.VMEM((NLAT, 2 * CH), BF16),
            pltpu.VMEM((NLAT, 2 * CH), BF16),
            pltpu.VMEM((NLAT, 2 * CH), BF16),
            pltpu.VMEM((NLAT, 2 * CH), F32),
            pltpu.VMEM((2 * NLAT, CH), BF16),
            dma((2, NG)),
            dma((9,)),
            dma((9, ND)),
            dma((9, ND)),
            dma((9,)),
            dma((9, NY)),
            dma((9, NY)),
            dma((3,)),
            dma((3,)),
            dma((3,)),
            dma((5, ND)),
            dma((5, ND)),
        ],
        compiler_params=pltpu.CompilerParams(
            collective_id=0, has_side_effects=True, vmem_limit_bytes=62 << 20
        ),
        cost_estimate=pl.CostEstimate(flops=10**10, bytes_accessed=3 * 10**7, transcendentals=10**6),
        name="spectral",
    )(fields, cotangent, tw, th, tht, w_first, w_second, bias)


def inverse_kernel(back_ref, cot_ref, twt_ref, grad_ref, bias_ref, out_ref, g1_ref, g2_ref, gb_ref, bs):
    xhi = lax.axis_index("lon")

    @pl.loop(0, NJ * ND)
    def _(jd):
        j, d = jd // ND, lax.rem(jd, ND)
        for ky in range(NY):
            rows = pl.ds(pl.multiple_of(jd * NY * SUB + ky * SUB, SUB), SUB)
            for ct in range(3):
                bs[ct, rows, :] = back_ref[j, d, ky, :, pl.ds(ct * 128, 128)].astype(F32)

    @pl.loop(0, GH)
    def _(h):
        spec = jnp.concatenate(
            [bs[ct, pl.ds(h, 2 * KW, stride=GH), :].astype(BF16) for ct in range(3)], 1
        )
        spatial = dot(twt_ref[xhi], spec) * LON_NORM
        out_ref[0, h] = (cot_ref[0, h].astype(F32) + spatial).astype(BF16)

    @pl.when(pl.program_id(0) == 0)
    def _():
        scale = 1.0 / math.sqrt(SPEC_ROWS)
        row = lax.broadcasted_iota(jnp.int32, (CH, BS), 0)
        col = lax.broadcasted_iota(jnp.int32, (CH, BS), 1)
        for m in range(2):
            pick = (row == col + (2 * xhi + m) * BS).astype(F32)

            def take(value):
                return scale * jnp.dot(
                    value, pick, precision=lax.Precision.HIGHEST, preferred_element_type=F32
                )

            for r in range(2):
                g1_ref[m, r] = take(grad_ref[r].reshape(BS, CH))
                g2_ref[m, r] = take(grad_ref[2 + r].reshape(BS, CH))
            gb_ref[m] = take(bias_ref[...])[:2]


def inverse_call(back, cotangent, twt, grads, bias):
    def whole(*shape):
        return pl.BlockSpec(shape, lambda g: (0,) * len(shape))

    return pl.pallas_call(
        inverse_kernel,
        grid=(NG,),
        out_shape=(
            jax.ShapeDtypeStruct((1, ROWS, HALF, CH), BF16),
            jax.ShapeDtypeStruct((2, 2, BS, BS), F32),
            jax.ShapeDtypeStruct((2, 2, BS, BS), F32),
            jax.ShapeDtypeStruct((2, 2, BS), F32),
        ),
        in_specs=[
            pl.BlockSpec((NJ, ND, NY, SUB, CH), lambda g: (0, 0, 0, g, 0)),
            pl.BlockSpec((1, GH, HALF, CH), lambda g: (0, g, 0, 0)),
            whole(2, HALF, 2 * KW),
            whole(NZ, NY, BS // NY, CH),
            whole(8, CH),
        ],
        out_specs=(
            pl.BlockSpec((1, GH, HALF, CH), lambda g: (0, g, 0, 0)),
            whole(2, 2, BS, BS),
            whole(2, 2, BS, BS),
            whole(2, 2, BS),
        ),
        scratch_shapes=[pltpu.VMEM((3, GH * 2 * KW, 128), F32)],
        compiler_params=pltpu.CompilerParams(vmem_limit_bytes=48 << 20),
        cost_estimate=pl.CostEstimate(
            flops=1400 * 10**6, bytes_accessed=18 * 10**6, transcendentals=0
        ),
        name="inverse",
    )(back, cotangent, twt, grads, bias)


def on_device(fields, cotangent, w_first, w_second, bias_first):
    tw, twt, th, tht = (jnp.asarray(table) for table in tables())
    back, grads, bias = spectral_call(
        fields, cotangent, tw, th, tht, w_first, w_second, bias_first
    )
    return inverse_call(back, cotangent, twt, grads, bias)


def solution(mesh):
    placed = (
        P("dp", "lat", "lon", None),
        P("dp", "lat", "lon", None),
        P("lon", None, None, None),
        P("lon", None, None, None),
        P("lon", None, None),
    )
    return jax.shard_map(
        on_device,
        mesh=mesh,
        in_specs=placed,
        out_specs=(
            P("dp", "lat", "lon", None),
            P("lon", None, None, None),
            P("lon", None, None, None),
            P("lon", None, None),
        ),
        check_vma=False,
    )
```

```python
import functools
import math

import jax
import jax.numpy as jnp
import numpy as np
from jax import lax
from jax.experimental import pallas as pl
from jax.experimental.pallas import tpu as pltpu
from jax.sharding import PartitionSpec as P

NLAT, NLON, KW, CH, BS, NBLK = 384, 768, 96, 384, 96, 4
HALF = NLON // 2
ROWS = 24
NG, GH = 3, 8
NJ = 3
ND = 8
NY = 4
NZ = 4
SUB = 2 * GH
WAVES = 2 * KW // NJ
BLK = NG * SUB
QROWS = 4 * BLK
SPEC_ROWS = 4 * NLAT * KW

LON_NORM = 1.0 / math.sqrt(NLON)
LAT_NORM = 1.0 / math.sqrt(NLAT)
shrink_level = 0.05
gelu_coef = 0.044715
root = math.sqrt(2.0 / math.pi)

MESH = pl.DeviceIdType.MESH
F32, BF16 = jnp.float32, jnp.bfloat16


def cos_sin(phase_int, period):
    phase = phase_int.astype(np.float32) * np.float32(2.0 * math.pi / period)
    return np.cos(phase).astype(np.float32), np.sin(phase).astype(np.float32)


def tables():
    kk = np.arange(KW, dtype=np.int64)[:, None]
    ww = np.arange(NLON, dtype=np.int64)[None, :]
    cosine, sine = cos_sin(kk * ww % NLON, NLON)
    tw = np.stack([cosine, -sine], 1).reshape(2 * KW, 2, HALF).transpose(1, 0, 2)
    pp = np.arange(NLAT, dtype=np.int64)[:, None]
    hh = np.arange(NLAT, dtype=np.int64)[None, :]
    cosine, sine = cos_sin(pp * hh % NLAT, NLAT)
    th = np.stack([np.stack([cosine, sine], 0), np.stack([-sine, cosine], 0)], 0)
    th = th.transpose(0, 2, 1, 3).reshape(2 * NLAT, 2, NLAT // ROWS, NG, GH)
    th = th.transpose(0, 2, 3, 1, 4).reshape(2 * NLAT, 2 * NLAT)
    kind = jnp.bfloat16
    return (
        tw.astype(kind),
        np.ascontiguousarray(tw.transpose(0, 2, 1)).astype(kind),
        th.astype(kind),
        np.ascontiguousarray(th.T).astype(kind),
    )


def dot(a, b):
    return jnp.dot(a, b, preferred_element_type=F32)


def dot_nt(a, b):
    return lax.dot_general(a, b, (((1,), (1,)), ((), ())), preferred_element_type=F32)


def dot_tn(a, b):
    return lax.dot_general(a, b, (((0,), (0,)), ((), ())), preferred_element_type=F32)


def spectral_kernel(
    f_hbm,
    c_hbm,
    tw_ref,
    th_ref,
    tht_ref,
    w1_ref,
    w2_ref,
    b1_ref,
    back_hbm,
    gout_ref,
    gbout_ref,
    w_all,
    b_all,
    wc1_ref,
    wc2_ref,
    bias_ref,
    gacc,
    gb_ref,
    gz,
    gzr,
    gy,
    gyr,
    gd,
    gdr,
    gyo,
    gzo,
    fbuf,
    cbuf,
    ps,
    xs,
    xr,
    ys,
    yr,
    yb,
    yrb,
    zbuf,
    hbuf,
    dobuf,
    dzbuf,
    gmbuf,
    dsbuf,
    ld_sem,
    xl_sem,
    xsend,
    xrecv,
    yl_sem,
    ysend,
    yrecv,
    wl_sem,
    wsend,
    wrecv,
    gsend,
    grecv,
):
    lat = lax.axis_index("lat")
    xhi = lax.axis_index("lon")
    dp = lax.axis_index("dp")
    y = lat // 4
    me = xhi * 4 + lax.rem(lat, 4)

    def device(yy, d, zz=dp):
        return (zz, yy * 4 + lax.rem(d, 4), d // 4)

    def load(which, g):
        src, dst = ((f_hbm, fbuf), (c_hbm, cbuf))[which]
        rows = pl.ds(g * GH, GH)
        return pltpu.make_async_copy(src.at[0, rows], dst.at[rows], ld_sem.at[which, g])

    for which in range(2):
        for g in range(NG):
            load(which, g).start()

    barrier = pltpu.get_barrier_semaphore()
    for i in range(1, ND):
        d = lax.rem(me + i, ND)
        pl.semaphore_signal(barrier, inc=1, device_id=device(y, d), device_id_type=MESH)
    for i in range(1, NY):
        yy = lax.rem(y + i, NY)
        pl.semaphore_signal(barrier, inc=1, device_id=device(yy, me), device_id_type=MESH)
    for i in range(1, NZ):
        zz = lax.rem(dp + i, NZ)
        pl.semaphore_signal(barrier, inc=1, device_id=device(y, me, zz), device_id_type=MESH)
    pl.semaphore_wait(barrier, ND - 1 + NY - 1 + NZ - 1)

    def weight_refs(i):
        return ((w1_ref, w_all.at[0, xhi]), (w2_ref, w_all.at[1, xhi]), (b1_ref, b_all.at[xhi]))[i]

    def weight_copy(i):
        src, dst = weight_refs(i)
        return pltpu.make_async_remote_copy(
            src_ref=src,
            dst_ref=dst,
            send_sem=wsend.at[i],
            recv_sem=wrecv.at[i],
            device_id=device(y, lax.rem(me + 4, ND)),
            device_id_type=MESH,
        )

    def weight_local(i):
        src, dst = weight_refs(i)
        return pltpu.make_async_copy(src, dst, wl_sem.at[i])

    def weights_start():
        for i in range(3):
            weight_copy(i).start()
            weight_local(i).start()

    def weights_build():
        for i in range(3):
            weight_copy(i).wait()
            weight_local(i).wait()
        row = lax.broadcasted_iota(jnp.int32, (BS, CH), 0)
        col = lax.broadcasted_iota(jnp.int32, (BS, CH), 1)
        bias = jnp.zeros((2, CH), F32)
        for n in range(NBLK):
            spread = col == row + n * BS
            bias += jnp.dot(
                b_all[n // 2, n % 2],
                spread.astype(F32),
                precision=lax.Precision.HIGHEST,
                preferred_element_type=F32,
            )
            spread = spread.astype(F32).astype(BF16)
            top, low = pl.ds(n * BS, BS), pl.ds(CH + n * BS, BS)
            re, im = pl.ds(0, CH), pl.ds(CH, CH)
            for i, out in enumerate((wc1_ref, wc2_ref)):
                real = dot(w_all[i, n // 2, n % 2, 0], spread)
                imag = dot(w_all[i, n // 2, n % 2, 1], spread)
                out[top, re] = real.astype(BF16)
                out[low, im] = real.astype(BF16)
                out[top, im] = imag.astype(BF16)
                out[low, re] = (-imag).astype(BF16)
        for r in range(2):
            bias_ref[:, pl.ds(r * CH, CH)] = bias[r : r + 1]

    def x_refs(slot, d, frm):
        if slot >= 9:
            return xs.at[0, 0, d, slot - 9], xr.at[0, 0, frm, slot - 9]
        if slot < 6:
            return xs.at[slot % 2, slot // 2, d], xr.at[slot % 2, slot // 2, frm]
        rows = pl.ds(pl.multiple_of(lax.rem(d, 4) * BLK, BLK), BLK)
        return yrb.at[slot - 6, :, rows], back_hbm.at[slot - 6, frm]

    def x_copy(slot, d, frm):
        src, dst = x_refs(slot, d, frm)
        return pltpu.make_async_remote_copy(
            src_ref=src,
            dst_ref=dst,
            send_sem=xsend.at[slot, d],
            recv_sem=xrecv.at[slot, frm],
            device_id=device(y, d),
            device_id_type=MESH,
        )

    def x_local(slot):
        src, dst = x_refs(slot, me, me)
        return pltpu.make_async_copy(src, dst, xl_sem.at[slot])

    def x_start(slot):
        @pl.loop(1, ND)
        def _(i):
            x_copy(slot, lax.rem(me + i, ND), me).start()

        x_local(slot).start()

    def x_wait_recv(slot):
        @pl.loop(1, ND)
        def _(i):
            frm = lax.rem(me + ND - i, ND)
            x_copy(slot, frm, frm).wait_recv()

        x_local(slot).wait()

    def x_wait_send(slot):
        @pl.loop(1, ND)
        def _(i):
            x_copy(slot, lax.rem(me + i, ND), me).wait_send()

    def y_refs(slot, yy, frm):
        if slot < 6:
            return ys.at[slot % 2, slot // 2, yy], yr.at[slot % 2, slot // 2, frm]
        return yb.at[slot - 6, yy], yrb.at[slot - 6, frm]

    def y_copy(slot, yy, frm):
        src, dst = y_refs(slot, yy, frm)
        return pltpu.make_async_remote_copy(
            src_ref=src,
            dst_ref=dst,
            send_sem=ysend.at[slot, yy],
            recv_sem=yrecv.at[slot, frm],
            device_id=device(yy, me),
            device_id_type=MESH,
        )

    def y_local(slot):
        src, dst = y_refs(slot, y, y)
        return pltpu.make_async_copy(src, dst, yl_sem.at[slot])

    def y_start(slot):
        @pl.loop(1, NY)
        def _(i):
            y_copy(slot, lax.rem(y + i, NY), y).start()

        y_local(slot).start()

    def y_wait_recv(slot):
        @pl.loop(1, NY)
        def _(i):
            frm = lax.rem(y + NY - i, NY)
            y_copy(slot, frm, frm).wait_recv()

        y_local(slot).wait()

    def y_wait_send(slot):
        @pl.loop(1, NY)
        def _(i):
            y_copy(slot, lax.rem(y + i, NY), y).wait_send()

    def lon_group(which, j, g):
        buf = (fbuf, cbuf)[which]
        left = tw_ref[xhi, pl.ds(j * WAVES, WAVES), :]
        for h in range(GH):
            part = dot(left, buf[g * GH + h])
            for ct in range(3):
                ps[ct, pl.ds(h * WAVES, WAVES), :] = part[:, ct * 128 : (ct + 1) * 128]
        for d in range(ND):
            for ky in range(NY):
                base = (d * NY + ky) * 2
                for ct in range(3):
                    tile = jnp.concatenate(
                        [ps[ct, pl.ds(base + r, GH, stride=WAVES), :] for r in range(2)], 0
                    )
                    xs[which, j, d, g, ky, :, pl.ds(ct * 128, 128)] = (tile * LON_NORM).astype(BF16)

    def lon_chunk(which, j):
        @pl.loop(0, NG)
        def _(g):
            lon_group(which, j, g)

        x_start(2 * j + which)

    def x_sum(which, j):
        @pl.loop(0, 4)
        def _(s):
            for g in range(NG):
                for ky in range(NY):
                    both = xr[which, j, s, g, ky].astype(F32) + xr[which, j, s + 4, g, ky].astype(F32)
                    rows = pl.ds(pl.multiple_of(s * BLK + g * SUB, SUB), SUB)
                    ys[which, j, ky, rows, :] = both.astype(BF16)

    def x_to_y(which, j):
        for slot in (9, 10, 11) if which == j == 0 else (2 * j + which,):
            x_wait_recv(slot)
        x_sum(which, j)
        y_start(2 * j + which)

    TILE = 192

    def spectral(j):
        wave = (j * ND + me) * NY + y
        doubling = jnp.where(wave == 0, 1.0, 2.0).astype(F32) * LAT_NORM

        @pl.loop(0, 2)
        def _(t):
            rows = pl.ds(pl.multiple_of(t * TILE, TILE), TILE)
            for q in range(2):
                trows = pl.ds(pl.multiple_of(q * NLAT + t * TILE, TILE), TILE)
                cols = pl.ds(q * CH, CH)
                left = th_ref[trows, :]
                zbuf[rows, cols] = (
                    dot(left, yr[0, j].reshape(2 * NLAT, CH)) * LAT_NORM
                ).astype(BF16)
                gmbuf[rows, cols] = dot(left, yr[1, j].reshape(2 * NLAT, CH)) * doubling

        @pl.loop(0, 2)
        def _(t):
            rows = pl.ds(pl.multiple_of(t * TILE, TILE), TILE)
            o1 = dot(zbuf[rows, :], wc1_ref[...]) + bias_ref[...]
            square = o1 * o1
            tangent = jnp.tanh(root * (o1 + gelu_coef * o1 * square))
            hbuf[rows, :] = (0.5 * o1 * (1.0 + tangent)).astype(BF16)
            slope = 0.5 * (1.0 + tangent) + 0.5 * o1 * (1.0 - tangent * tangent) * root * (
                1.0 + 3.0 * gelu_coef * square
            )
            o2 = dot(hbuf[rows, :], wc2_ref[...])
            square = o2 * o2
            keep = square / (square + shrink_level * shrink_level)
            dobuf[rows, :] = (keep * gmbuf[rows, :]).astype(BF16)
            dh = dot_nt(dobuf[rows, :], wc2_ref[...])
            dz = (slope * dh).astype(BF16)
            dzbuf[rows, :] = dz
            gb_ref[...] += jnp.sum(dz.astype(F32), 0, keepdims=True)
            ds = dot_nt(dz, wc1_ref[...]).astype(BF16)
            for q in range(2):
                trows = pl.ds(pl.multiple_of(q * NLAT + t * TILE, TILE), TILE)
                dsbuf[trows, :] = ds[:, q * CH : (q + 1) * CH]

        @pl.loop(0, NY)
        def _(yy):
            rows = pl.ds(pl.multiple_of(yy * QROWS, QROWS), QROWS)
            yb[j, yy] = (dot(tht_ref[rows, :], dsbuf[...]) * LAT_NORM).astype(BF16)

        y_start(6 + j)

        re, im = pl.ds(0, CH), pl.ds(CH, CH)
        for i, (zz, dd) in enumerate(((zbuf, dzbuf), (hbuf, dobuf))):
            gacc[2 * i] += dot_tn(zz[:, re], dd[:, re]) + dot_tn(zz[:, im], dd[:, im])
            gacc[2 * i + 1] += dot_tn(zz[:, re], dd[:, im]) - dot_tn(zz[:, im], dd[:, re])

    def grad_copy(stage, to, frm):
        src, dst, target = (
            lambda: (gz.at[to], gzr.at[frm], device(y, me, to)),
            lambda: (gy.at[to], gyr.at[frm], device(to, me)),
            lambda: (gd, gdr.at[frm], device(y, to)),
            lambda: (gd.at[pl.ds(0, BS // NY)], gyo.at[frm], device(to, me)),
            lambda: (gyo, gzo.at[frm], device(y, me, to)),
        )[stage]()
        return pltpu.make_async_remote_copy(
            src_ref=src,
            dst_ref=dst,
            send_sem=gsend.at[stage, to],
            recv_sem=grecv.at[stage, frm],
            device_id=target,
            device_id_type=MESH,
        )

    stage_size = (NZ, NY, ND, NY, NZ)
    stage_place = (dp, y, me, y, dp)

    def grad_start(stage):
        here, size = stage_place[stage], stage_size[stage]

        @pl.loop(1, size)
        def _(i):
            grad_copy(stage, lax.rem(here + i, size), here).start()

    def grad_wait(stage):
        here, size = stage_place[stage], stage_size[stage]

        @pl.loop(1, size)
        def _(i):
            frm = lax.rem(here + size - i, size)
            grad_copy(stage, frm, frm).wait_recv()

        @pl.loop(1, size)
        def _(i):
            grad_copy(stage, lax.rem(here + i, size), here).wait_send()

    def grad_begin():
        lane = lax.broadcasted_iota(jnp.int32, (BS, CH), 1)
        line = lax.broadcasted_iota(jnp.int32, (8, CH), 0)
        both = [jnp.broadcast_to(gb_ref[:, pl.ds(r * CH, CH)], (8, CH)) for r in range(2)]
        sums = jnp.where(line == 0, both[0], jnp.where(line == 1, both[1], 0.0))
        for i in range(NZ):
            part = gacc[i, pl.ds(0, BS), :]
            for n in range(1, NBLK):
                part = jnp.where(lane >= n * BS, gacc[i, pl.ds(n * BS, BS), :], part)
            gz[i, pl.ds(0, BS), :] = part
            gz[i, pl.ds(BS, 8), :] = sums
        gzr[dp] = gz[dp]
        grad_start(0)

    def grad_finish(after_exchange_starts):
        part = BS // NY
        grad_wait(0)
        total = gzr[0] + gzr[1] + gzr[2] + gzr[3]
        for i in range(NY):
            gy[i, pl.ds(0, part), :] = total[i * part : (i + 1) * part]
            gy[i, pl.ds(part, 8), :] = total[BS:]
        gyr[y] = gy[y]
        grad_start(1)
        grad_wait(1)
        gd[...] = gyr[0] + gyr[1] + gyr[2] + gyr[3]
        gdr[me] = gd[...]
        grad_start(2)
        after_exchange_starts()
        grad_wait(2)
        total = gdr[0]
        for i in range(1, ND):
            total += gdr[i]
        gd[...] = total
        gbout_ref[...] = total[part:]
        gyo[y] = total[:part]
        grad_start(3)
        grad_wait(3)
        gzo[dp] = gyo[...]
        grad_start(4)
        grad_wait(4)
        gout_ref[...] = gzo[...]

    weights_start()
    for g in range(NG):
        load(0, g).wait()
        lon_group(0, 0, g)
        x_start(9 + g)
    for g in range(NG):
        load(1, g).wait()
    lon_chunk(1, 0)
    gacc[...] = jnp.zeros_like(gacc)
    gb_ref[...] = jnp.zeros_like(gb_ref)
    for j in range(1, NJ):
        lon_chunk(0, j)
        lon_chunk(1, j)
    weights_build()

    for j in range(NJ):
        x_to_y(0, j)
        x_to_y(1, j)
        if j > 0:
            y_wait_recv(5 + j)
            x_start(5 + j)
        y_wait_recv(2 * j)
        y_wait_recv(2 * j + 1)
        spectral(j)
    grad_begin()
    grad_finish(lambda: (y_wait_recv(8), x_start(8)))
    for slot in range(6, 9):
        x_wait_recv(slot)
    for slot in range(1, 12):
        x_wait_send(slot)
    for slot in range(9):
        y_wait_send(slot)


def spectral_call(fields, cotangent, tw, th, tht, w_first, w_second, bias):
    vm = pl.BlockSpec(memory_space=pltpu.VMEM)
    hbm = pl.BlockSpec(memory_space=pl.ANY)
    dma = pltpu.SemaphoreType.DMA
    return pl.pallas_call(
        spectral_kernel,
        out_shape=(
            jax.ShapeDtypeStruct((NJ, ND, NY, BLK, CH), BF16),
            jax.ShapeDtypeStruct((NZ, NY, BS // NY, CH), F32),
            jax.ShapeDtypeStruct((8, CH), F32),
        ),
        in_specs=[hbm, hbm] + [vm] * 6,
        out_specs=(hbm, vm, vm),
        scratch_shapes=[
            pltpu.VMEM((2, 2, 2, 2, BS, BS), BF16),
            pltpu.VMEM((2, 2, 2, BS), F32),
            pltpu.VMEM((2 * CH, 2 * CH), BF16),
            pltpu.VMEM((2 * CH, 2 * CH), BF16),
            pltpu.VMEM((1, 2 * CH), F32),
            pltpu.VMEM((4, CH, CH), F32),
            pltpu.VMEM((1, 2 * CH), F32),
            pltpu.VMEM((NZ, BS + 8, CH), F32),
            pltpu.VMEM((NZ, BS + 8, CH), F32),
            pltpu.VMEM((NY, BS // NY + 8, CH), F32),
            pltpu.VMEM((NY, BS // NY + 8, CH), F32),
            pltpu.VMEM((BS // NY + 8, CH), F32),
            pltpu.VMEM((ND, BS // NY + 8, CH), F32),
            pltpu.VMEM((NY, BS // NY, CH), F32),
            pltpu.VMEM((NZ, NY, BS // NY, CH), F32),
            pltpu.VMEM((ROWS, HALF, CH), BF16),
            pltpu.VMEM((ROWS, HALF, CH), BF16),
            pltpu.VMEM((3, GH * WAVES, 128), F32),
            pltpu.VMEM((2, NJ, ND, NG, NY, SUB, CH), BF16),
            pltpu.VMEM((2, NJ, ND, NG, NY, SUB, CH), BF16),
            pltpu.VMEM((2, NJ, NY, QROWS, CH), BF16),
            pltpu.VMEM((2, NJ, NY, QROWS, CH), BF16),
            pltpu.VMEM((NJ, NY, QROWS, CH), BF16),
            pltpu.VMEM((NJ, NY, QROWS, CH), BF16),
            pltpu.VMEM((NLAT, 2 * CH), BF16),
            pltpu.VMEM((NLAT, 2 * CH), BF16),
            pltpu.VMEM((NLAT, 2 * CH), BF16),
            pltpu.VMEM((NLAT, 2 * CH), BF16),
            pltpu.VMEM((NLAT, 2 * CH), F32),
            pltpu.VMEM((2 * NLAT, CH), BF16),
            dma((2, NG)),
            dma((12,)),
            dma((12, ND)),
            dma((12, ND)),
            dma((9,)),
            dma((9, NY)),
            dma((9, NY)),
            dma((3,)),
            dma((3,)),
            dma((3,)),
            dma((5, ND)),
            dma((5, ND)),
        ],
        compiler_params=pltpu.CompilerParams(
            collective_id=0, has_side_effects=True, vmem_limit_bytes=62 << 20
        ),
        cost_estimate=pl.CostEstimate(flops=10**10, bytes_accessed=3 * 10**7, transcendentals=10**6),
        name="spectral",
    )(fields, cotangent, tw, th, tht, w_first, w_second, bias)


def inverse_kernel(back_ref, cot_ref, twt_ref, grad_ref, bias_ref, out_ref, g1_ref, g2_ref, gb_ref, bs):
    xhi = lax.axis_index("lon")

    @pl.loop(0, NJ * ND)
    def _(jd):
        j, d = jd // ND, lax.rem(jd, ND)
        for ky in range(NY):
            rows = pl.ds(pl.multiple_of(jd * NY * SUB + ky * SUB, SUB), SUB)
            for ct in range(3):
                bs[ct, rows, :] = back_ref[j, d, ky, :, pl.ds(ct * 128, 128)].astype(F32)

    @pl.loop(0, GH)
    def _(h):
        spec = jnp.concatenate(
            [bs[ct, pl.ds(h, 2 * KW, stride=GH), :].astype(BF16) for ct in range(3)], 1
        )
        spatial = dot(twt_ref[xhi], spec) * LON_NORM
        out_ref[0, h] = (cot_ref[0, h].astype(F32) + spatial).astype(BF16)

    @pl.when(pl.program_id(0) == 0)
    def _():
        scale = 1.0 / math.sqrt(SPEC_ROWS)
        row = lax.broadcasted_iota(jnp.int32, (CH, BS), 0)
        col = lax.broadcasted_iota(jnp.int32, (CH, BS), 1)
        for m in range(2):
            pick = (row == col + (2 * xhi + m) * BS).astype(F32)

            def take(value):
                return scale * jnp.dot(
                    value, pick, precision=lax.Precision.HIGHEST, preferred_element_type=F32
                )

            for r in range(2):
                g1_ref[m, r] = take(grad_ref[r].reshape(BS, CH))
                g2_ref[m, r] = take(grad_ref[2 + r].reshape(BS, CH))
            gb_ref[m] = take(bias_ref[...])[:2]


def inverse_call(back, cotangent, twt, grads, bias):
    def whole(*shape):
        return pl.BlockSpec(shape, lambda g: (0,) * len(shape))

    return pl.pallas_call(
        inverse_kernel,
        grid=(NG,),
        out_shape=(
            jax.ShapeDtypeStruct((1, ROWS, HALF, CH), BF16),
            jax.ShapeDtypeStruct((2, 2, BS, BS), F32),
            jax.ShapeDtypeStruct((2, 2, BS, BS), F32),
            jax.ShapeDtypeStruct((2, 2, BS), F32),
        ),
        in_specs=[
            pl.BlockSpec((NJ, ND, NY, SUB, CH), lambda g: (0, 0, 0, g, 0)),
            pl.BlockSpec((1, GH, HALF, CH), lambda g: (0, g, 0, 0)),
            whole(2, HALF, 2 * KW),
            whole(NZ, NY, BS // NY, CH),
            whole(8, CH),
        ],
        out_specs=(
            pl.BlockSpec((1, GH, HALF, CH), lambda g: (0, g, 0, 0)),
            whole(2, 2, BS, BS),
            whole(2, 2, BS, BS),
            whole(2, 2, BS),
        ),
        scratch_shapes=[pltpu.VMEM((3, GH * 2 * KW, 128), F32)],
        compiler_params=pltpu.CompilerParams(vmem_limit_bytes=62 << 20),
        cost_estimate=pl.CostEstimate(
            flops=1400 * 10**6, bytes_accessed=18 * 10**6, transcendentals=0
        ),
        name="inverse",
    )(back, cotangent, twt, grads, bias)


def on_device(fields, cotangent, w_first, w_second, bias_first):
    tw, twt, th, tht = (jnp.asarray(table) for table in tables())
    back, grads, bias = spectral_call(
        fields, cotangent, tw, th, tht, w_first, w_second, bias_first
    )
    return inverse_call(back, cotangent, twt, grads, bias)


def solution(mesh):
    placed = (
        P("dp", "lat", "lon", None),
        P("dp", "lat", "lon", None),
        P("lon", None, None, None),
        P("lon", None, None, None),
        P("lon", None, None),
    )
    return jax.shard_map(
        on_device,
        mesh=mesh,
        in_specs=placed,
        out_specs=(
            P("dp", "lat", "lon", None),
            P("lon", None, None, None),
            P("lon", None, None, None),
            P("lon", None, None),
        ),
        check_vma=False,
    )
```

```python
import functools
import math

import jax
import jax.numpy as jnp
import numpy as np
from jax import lax
from jax.experimental import pallas as pl
from jax.experimental.pallas import tpu as pltpu
from jax.sharding import PartitionSpec as P

NLAT, NLON, KW, CH, BS, NBLK = 384, 768, 96, 384, 96, 4
HALF = NLON // 2
ROWS = 24
NG, GH = 3, 8
NJ = 3
ND = 8
NY = 4
NZ = 4
LANES = 256
SUB = 2 * GH
WAVES = 2 * KW // NJ
BLK = NG * SUB
QROWS = 4 * BLK
SPEC_ROWS = 4 * NLAT * KW

LON_NORM = 1.0 / math.sqrt(NLON)
LAT_NORM = 1.0 / math.sqrt(NLAT)
shrink_level = 0.05
gelu_coef = 0.044715
root = math.sqrt(2.0 / math.pi)

MESH = pl.DeviceIdType.MESH
F32, BF16 = jnp.float32, jnp.bfloat16


def cos_sin(phase_int, period):
    phase = phase_int.astype(np.float32) * np.float32(2.0 * math.pi / period)
    return np.cos(phase).astype(np.float32), np.sin(phase).astype(np.float32)


def tables():
    kk = np.arange(KW, dtype=np.int64)[:, None]
    ww = np.arange(NLON, dtype=np.int64)[None, :]
    cosine, sine = cos_sin(kk * ww % NLON, NLON)
    tw = np.stack([cosine, -sine], 1).reshape(2 * KW, 2, HALF).transpose(1, 0, 2)
    pp = np.arange(NLAT, dtype=np.int64)[:, None]
    hh = np.arange(NLAT, dtype=np.int64)[None, :]
    cosine, sine = cos_sin(pp * hh % NLAT, NLAT)
    th = np.stack([np.stack([cosine, sine], 0), np.stack([-sine, cosine], 0)], 0)
    th = th.transpose(0, 2, 1, 3).reshape(2 * NLAT, 2, NLAT // ROWS, NG, GH)
    th = th.transpose(0, 2, 3, 1, 4).reshape(2 * NLAT, 2 * NLAT)
    kind = jnp.bfloat16
    return (
        tw.astype(kind),
        np.ascontiguousarray(tw.transpose(0, 2, 1)).astype(kind),
        th.astype(kind),
        np.ascontiguousarray(th.T).astype(kind),
    )


def dot(a, b):
    return jnp.dot(a, b, preferred_element_type=F32)


def dot_nt(a, b):
    return lax.dot_general(a, b, (((1,), (1,)), ((), ())), preferred_element_type=F32)


def dot_tn(a, b):
    return lax.dot_general(a, b, (((0,), (0,)), ((), ())), preferred_element_type=F32)


def spectral_kernel(
    f_hbm,
    c_hbm,
    tw_ref,
    th_ref,
    tht_ref,
    w1_ref,
    w2_ref,
    b1_ref,
    back_hbm,
    gout_ref,
    gbout_ref,
    w_all,
    b_all,
    wc1_ref,
    wc2_ref,
    bias_ref,
    gacc,
    gb_ref,
    gz,
    gzr,
    gy,
    gyr,
    gd,
    gdr,
    gyo,
    gzo,
    fbuf,
    cbuf,
    ps,
    xs,
    xr,
    ys,
    yr,
    yb,
    yrb,
    zbuf,
    hbuf,
    dobuf,
    dzbuf,
    gmbuf,
    dsbuf,
    ld_sem,
    xl_sem,
    xsend,
    xrecv,
    yl_sem,
    ysend,
    yrecv,
    wl_sem,
    wsend,
    wrecv,
    gsend,
    grecv,
):
    lat = lax.axis_index("lat")
    xhi = lax.axis_index("lon")
    dp = lax.axis_index("dp")
    y = lat // 4
    me = xhi * 4 + lax.rem(lat, 4)

    def device(yy, d, zz=dp):
        return (zz, yy * 4 + lax.rem(d, 4), d // 4)

    def load(which, g):
        src, dst = ((f_hbm, fbuf), (c_hbm, cbuf))[which]
        rows = pl.ds(g * GH, GH)
        return pltpu.make_async_copy(src.at[0, rows], dst.at[rows], ld_sem.at[which, g])

    for which in range(2):
        for g in range(NG):
            load(which, g).start()

    barrier = pltpu.get_barrier_semaphore()
    for i in range(1, ND):
        d = lax.rem(me + i, ND)
        pl.semaphore_signal(barrier, inc=1, device_id=device(y, d), device_id_type=MESH)
    for i in range(1, NY):
        yy = lax.rem(y + i, NY)
        pl.semaphore_signal(barrier, inc=1, device_id=device(yy, me), device_id_type=MESH)
    for i in range(1, NZ):
        zz = lax.rem(dp + i, NZ)
        pl.semaphore_signal(barrier, inc=1, device_id=device(y, me, zz), device_id_type=MESH)
    pl.semaphore_wait(barrier, ND - 1 + NY - 1 + NZ - 1)

    def weight_refs(i):
        return ((w1_ref, w_all.at[0, xhi]), (w2_ref, w_all.at[1, xhi]), (b1_ref, b_all.at[xhi]))[i]

    def weight_copy(i):
        src, dst = weight_refs(i)
        return pltpu.make_async_remote_copy(
            src_ref=src,
            dst_ref=dst,
            send_sem=wsend.at[i],
            recv_sem=wrecv.at[i],
            device_id=device(y, lax.rem(me + 4, ND)),
            device_id_type=MESH,
        )

    def weight_local(i):
        src, dst = weight_refs(i)
        return pltpu.make_async_copy(src, dst, wl_sem.at[i])

    def weights_start():
        for i in range(3):
            weight_copy(i).start()
            weight_local(i).start()

    def weights_build():
        for i in range(3):
            weight_copy(i).wait()
            weight_local(i).wait()
        row = lax.broadcasted_iota(jnp.int32, (BS, CH), 0)
        col = lax.broadcasted_iota(jnp.int32, (BS, CH), 1)
        bias = jnp.zeros((2, CH), F32)
        for n in range(NBLK):
            spread = col == row + n * BS
            bias += jnp.dot(
                b_all[n // 2, n % 2],
                spread.astype(F32),
                precision=lax.Precision.HIGHEST,
                preferred_element_type=F32,
            )
            spread = spread.astype(F32).astype(BF16)
            top, low = pl.ds(n * BS, BS), pl.ds(CH + n * BS, BS)
            re, im = pl.ds(0, CH), pl.ds(CH, CH)
            for i, out in enumerate((wc1_ref, wc2_ref)):
                real = dot(w_all[i, n // 2, n % 2, 0], spread)
                imag = dot(w_all[i, n // 2, n % 2, 1], spread)
                out[top, re] = real.astype(BF16)
                out[low, im] = real.astype(BF16)
                out[top, im] = imag.astype(BF16)
                out[low, re] = (-imag).astype(BF16)
        for r in range(2):
            bias_ref[:, pl.ds(r * CH, CH)] = bias[r : r + 1]

    def x_refs(slot, d, frm):
        if slot >= 15:
            return xs.at[0, 0, d, slot - 15], xr.at[0, 0, frm, slot - 15]
        if slot < 6:
            return xs.at[slot % 2, slot // 2, d], xr.at[slot % 2, slot // 2, frm]
        j, g = (slot - 6) // NG, (slot - 6) % NG
        rows = pl.ds(pl.multiple_of(lax.rem(d, 4) * BLK + g * SUB, SUB), SUB)
        return yrb.at[j, :, rows], back_hbm.at[g, j, frm]

    def x_copy(slot, d, frm):
        src, dst = x_refs(slot, d, frm)
        return pltpu.make_async_remote_copy(
            src_ref=src,
            dst_ref=dst,
            send_sem=xsend.at[slot, d],
            recv_sem=xrecv.at[slot, frm],
            device_id=device(y, d),
            device_id_type=MESH,
        )

    def x_local(slot):
        src, dst = x_refs(slot, me, me)
        return pltpu.make_async_copy(src, dst, xl_sem.at[slot])

    def x_start(slot):
        @pl.loop(1, ND)
        def _(i):
            x_copy(slot, lax.rem(me + i, ND), me).start()

        x_local(slot).start()

    def x_wait_recv(slot):
        @pl.loop(1, ND)
        def _(i):
            frm = lax.rem(me + ND - i, ND)
            x_copy(slot, frm, frm).wait_recv()

        x_local(slot).wait()

    def x_wait_send(slot):
        @pl.loop(1, ND)
        def _(i):
            x_copy(slot, lax.rem(me + i, ND), me).wait_send()

    def y_refs(slot, yy, frm):
        if slot < 6:
            return ys.at[slot % 2, slot // 2, yy], yr.at[slot % 2, slot // 2, frm]
        return yb.at[slot - 6, yy], yrb.at[slot - 6, frm]

    def y_copy(slot, yy, frm):
        src, dst = y_refs(slot, yy, frm)
        return pltpu.make_async_remote_copy(
            src_ref=src,
            dst_ref=dst,
            send_sem=ysend.at[slot, yy],
            recv_sem=yrecv.at[slot, frm],
            device_id=device(yy, me),
            device_id_type=MESH,
        )

    def y_local(slot):
        src, dst = y_refs(slot, y, y)
        return pltpu.make_async_copy(src, dst, yl_sem.at[slot])

    def y_start(slot):
        @pl.loop(1, NY)
        def _(i):
            y_copy(slot, lax.rem(y + i, NY), y).start()

        y_local(slot).start()

    def y_wait_recv(slot):
        @pl.loop(1, NY)
        def _(i):
            frm = lax.rem(y + NY - i, NY)
            y_copy(slot, frm, frm).wait_recv()

        y_local(slot).wait()

    def y_wait_send(slot):
        @pl.loop(1, NY)
        def _(i):
            y_copy(slot, lax.rem(y + i, NY), y).wait_send()

    def lon_group(which, j, g):
        buf = (fbuf, cbuf)[which]
        left = tw_ref[xhi, pl.ds(j * WAVES, WAVES), :]
        for h in range(GH):
            part = dot(left, buf[g * GH + h])
            for ct in range(3):
                ps[ct, pl.ds(h * WAVES, WAVES), :] = part[:, ct * 128 : (ct + 1) * 128]

        @pl.loop(0, ND)
        def _(d):
            for ky in range(NY):
                base = (d * NY + ky) * 2
                for ct in range(3):
                    tile = jnp.concatenate(
                        [ps[ct, pl.ds(base + r, GH, stride=WAVES), :] for r in range(2)], 0
                    )
                    xs[which, j, d, g, ky, :, pl.ds(ct * 128, 128)] = (tile * LON_NORM).astype(BF16)

    def lon_chunk(which, j):
        @pl.loop(0, NG)
        def _(g):
            lon_group(which, j, g)

        x_start(2 * j + which)

    def x_sum(which, j):
        @pl.loop(0, 4)
        def _(s):
            for g in range(NG):
                for ky in range(NY):
                    both = xr[which, j, s, g, ky].astype(F32) + xr[which, j, s + 4, g, ky].astype(F32)
                    rows = pl.ds(pl.multiple_of(s * BLK + g * SUB, SUB), SUB)
                    ys[which, j, ky, rows, :] = both.astype(BF16)

    def x_to_y(which, j):
        for slot in (15, 16, 17) if which == j == 0 else (2 * j + which,):
            x_wait_recv(slot)
        x_sum(which, j)
        y_start(2 * j + which)

    TILE = 192

    def spectral(j):
        wave = (j * ND + me) * NY + y
        doubling = jnp.where(wave == 0, 1.0, 2.0).astype(F32) * LAT_NORM

        @pl.loop(0, 2)
        def _(t):
            rows = pl.ds(pl.multiple_of(t * TILE, TILE), TILE)
            for q in range(2):
                trows = pl.ds(pl.multiple_of(q * NLAT + t * TILE, TILE), TILE)
                cols = pl.ds(q * CH, CH)
                left = th_ref[trows, :]
                zbuf[rows, cols] = (
                    dot(left, yr[0, j].reshape(2 * NLAT, CH)) * LAT_NORM
                ).astype(BF16)
                gmbuf[rows, cols] = dot(left, yr[1, j].reshape(2 * NLAT, CH)) * doubling

        @pl.loop(0, 2)
        def _(t):
            rows = pl.ds(pl.multiple_of(t * TILE, TILE), TILE)
            o1 = dot(zbuf[rows, :], wc1_ref[...]) + bias_ref[...]
            square = o1 * o1
            tangent = jnp.tanh(root * (o1 + gelu_coef * o1 * square))
            hbuf[rows, :] = (0.5 * o1 * (1.0 + tangent)).astype(BF16)
            slope = 0.5 * (1.0 + tangent) + 0.5 * o1 * (1.0 - tangent * tangent) * root * (
                1.0 + 3.0 * gelu_coef * square
            )
            o2 = dot(hbuf[rows, :], wc2_ref[...])
            square = o2 * o2
            keep = square / (square + shrink_level * shrink_level)
            dobuf[rows, :] = (keep * gmbuf[rows, :]).astype(BF16)
            dh = dot_nt(dobuf[rows, :], wc2_ref[...])
            dz = (slope * dh).astype(BF16)
            dzbuf[rows, :] = dz
            gb_ref[...] += jnp.sum(dz.astype(F32), 0, keepdims=True)
            ds = dot_nt(dz, wc1_ref[...]).astype(BF16)
            for q in range(2):
                trows = pl.ds(pl.multiple_of(q * NLAT + t * TILE, TILE), TILE)
                dsbuf[trows, :] = ds[:, q * CH : (q + 1) * CH]

        re, im = pl.ds(0, CH), pl.ds(CH, CH)
        for i, (zz, dd) in enumerate(((zbuf, dzbuf), (hbuf, dobuf))):
            gacc[2 * i] += dot_tn(zz[:, re], dd[:, re]) + dot_tn(zz[:, im], dd[:, im])
            gacc[2 * i + 1] += dot_tn(zz[:, re], dd[:, im]) - dot_tn(zz[:, im], dd[:, re])
        if j == NJ - 1:
            grad_begin()

        @pl.loop(0, NY)
        def _(yy):
            rows = pl.ds(pl.multiple_of(yy * QROWS, QROWS), QROWS)
            yb[j, yy] = (dot(tht_ref[rows, :], dsbuf[...]) * LAT_NORM).astype(BF16)

        y_start(6 + j)

    def grad_copy(stage, to, frm):
        src, dst, target = (
            lambda: (gz.at[to], gzr.at[frm], device(y, me, to)),
            lambda: (gy.at[to], gyr.at[frm], device(to, me)),
            lambda: (gd, gdr.at[frm], device(y, to)),
            lambda: (gd.at[pl.ds(0, BS // NY), lanes], gyo.at[frm], device(to, me)),
            lambda: (gyo, gzo.at[frm], device(y, me, to)),
        )[stage]()
        return pltpu.make_async_remote_copy(
            src_ref=src,
            dst_ref=dst,
            send_sem=gsend.at[stage, to],
            recv_sem=grecv.at[stage, frm],
            device_id=target,
            device_id_type=MESH,
        )

    lanes = pl.ds(pl.multiple_of(xhi * 128, 128), LANES)
    stage_size = (NZ, NY, ND, NY, NZ)
    stage_place = (dp, y, me, y, dp)

    def grad_start(stage):
        here, size = stage_place[stage], stage_size[stage]

        @pl.loop(1, size)
        def _(i):
            grad_copy(stage, lax.rem(here + i, size), here).start()

    def grad_wait(stage):
        here, size = stage_place[stage], stage_size[stage]

        @pl.loop(1, size)
        def _(i):
            frm = lax.rem(here + size - i, size)
            grad_copy(stage, frm, frm).wait_recv()

        @pl.loop(1, size)
        def _(i):
            grad_copy(stage, lax.rem(here + i, size), here).wait_send()

    def grad_begin():
        lane = lax.broadcasted_iota(jnp.int32, (BS, CH), 1)
        line = lax.broadcasted_iota(jnp.int32, (8, CH), 0)
        both = [jnp.broadcast_to(gb_ref[:, pl.ds(r * CH, CH)], (8, CH)) for r in range(2)]
        sums = jnp.where(line == 0, both[0], jnp.where(line == 1, both[1], 0.0))
        for i in range(NZ):
            part = gacc[i, pl.ds(0, BS), :]
            for n in range(1, NBLK):
                part = jnp.where(lane >= n * BS, gacc[i, pl.ds(n * BS, BS), :], part)
            gz[i, pl.ds(0, BS), :] = part
            gz[i, pl.ds(BS, 8), :] = sums
        gzr[dp] = gz[dp]
        grad_start(0)

    def grad_finish(before_exchange, after_exchange_starts):
        part = BS // NY
        grad_wait(0)
        total = gzr[0] + gzr[1] + gzr[2] + gzr[3]
        for i in range(NY):
            gy[i, pl.ds(0, part), :] = total[i * part : (i + 1) * part]
            gy[i, pl.ds(part, 8), :] = total[BS:]
        gyr[y] = gy[y]
        grad_start(1)
        before_exchange()
        grad_wait(1)
        gd[...] = gyr[0] + gyr[1] + gyr[2] + gyr[3]
        gdr[me] = gd[...]
        grad_start(2)
        after_exchange_starts()
        grad_wait(2)
        total = gdr[0]
        for i in range(1, ND):
            total += gdr[i]
        gd[...] = total
        gbout_ref[...] = gd[pl.ds(part, 8), lanes]
        gyo[y] = gd[pl.ds(0, part), lanes]
        grad_start(3)
        grad_wait(3)
        gzo[dp] = gyo[...]
        grad_start(4)
        grad_wait(4)
        gout_ref[...] = gzo[...]

    weights_start()
    for g in range(NG):
        load(0, g).wait()
        lon_group(0, 0, g)
        x_start(15 + g)
    for g in range(NG):
        load(1, g).wait()
    lon_chunk(1, 0)
    gacc[...] = jnp.zeros_like(gacc)
    gb_ref[...] = jnp.zeros_like(gb_ref)
    for j in range(1, NJ):
        lon_chunk(0, j)
        lon_chunk(1, j)
    weights_build()

    for j in range(NJ):
        x_to_y(0, j)
        x_to_y(1, j)
        if j > 0:
            y_wait_recv(5 + j)
            for g in range(NG if j < NJ - 1 else NG - 1):
                x_start(6 + (j - 1) * NG + g)
        y_wait_recv(2 * j)
        y_wait_recv(2 * j + 1)
        spectral(j)

    def last_return():
        y_wait_recv(8)
        for g in range(NG):
            x_start(12 + g)

    grad_finish(lambda: x_start(11), last_return)
    for slot in range(6, 15):
        x_wait_recv(slot)
    for slot in range(1, 18):
        x_wait_send(slot)
    for slot in range(9):
        y_wait_send(slot)


def spectral_call(fields, cotangent, tw, th, tht, w_first, w_second, bias):
    vm = pl.BlockSpec(memory_space=pltpu.VMEM)
    hbm = pl.BlockSpec(memory_space=pl.ANY)
    dma = pltpu.SemaphoreType.DMA
    return pl.pallas_call(
        spectral_kernel,
        out_shape=(
            jax.ShapeDtypeStruct((NG, NJ, ND, NY, SUB, CH), BF16),
            jax.ShapeDtypeStruct((NZ, NY, BS // NY, LANES), F32),
            jax.ShapeDtypeStruct((8, LANES), F32),
        ),
        in_specs=[hbm, hbm] + [vm] * 6,
        out_specs=(hbm, vm, vm),
        scratch_shapes=[
            pltpu.VMEM((2, 2, 2, 2, BS, BS), BF16),
            pltpu.VMEM((2, 2, 2, BS), F32),
            pltpu.VMEM((2 * CH, 2 * CH), BF16),
            pltpu.VMEM((2 * CH, 2 * CH), BF16),
            pltpu.VMEM((1, 2 * CH), F32),
            pltpu.VMEM((4, CH, CH), F32),
            pltpu.VMEM((1, 2 * CH), F32),
            pltpu.VMEM((NZ, BS + 8, CH), F32),
            pltpu.VMEM((NZ, BS + 8, CH), F32),
            pltpu.VMEM((NY, BS // NY + 8, CH), F32),
            pltpu.VMEM((NY, BS // NY + 8, CH), F32),
            pltpu.VMEM((BS // NY + 8, CH), F32),
            pltpu.VMEM((ND, BS // NY + 8, CH), F32),
            pltpu.VMEM((NY, BS // NY, LANES), F32),
            pltpu.VMEM((NZ, NY, BS // NY, LANES), F32),
            pltpu.VMEM((ROWS, HALF, CH), BF16),
            pltpu.VMEM((ROWS, HALF, CH), BF16),
            pltpu.VMEM((3, GH * WAVES, 128), F32),
            pltpu.VMEM((2, NJ, ND, NG, NY, SUB, CH), BF16),
            pltpu.VMEM((2, NJ, ND, NG, NY, SUB, CH), BF16),
            pltpu.VMEM((2, NJ, NY, QROWS, CH), BF16),
            pltpu.VMEM((2, NJ, NY, QROWS, CH), BF16),
            pltpu.VMEM((NJ, NY, QROWS, CH), BF16),
            pltpu.VMEM((NJ, NY, QROWS, CH), BF16),
            pltpu.VMEM((NLAT, 2 * CH), BF16),
            pltpu.VMEM((NLAT, 2 * CH), BF16),
            pltpu.VMEM((NLAT, 2 * CH), BF16),
            pltpu.VMEM((NLAT, 2 * CH), BF16),
            pltpu.VMEM((NLAT, 2 * CH), F32),
            pltpu.VMEM((2 * NLAT, CH), BF16),
            dma((2, NG)),
            dma((18,)),
            dma((18, ND)),
            dma((18, ND)),
            dma((9,)),
            dma((9, NY)),
            dma((9, NY)),
            dma((3,)),
            dma((3,)),
            dma((3,)),
            dma((5, ND)),
            dma((5, ND)),
        ],
        compiler_params=pltpu.CompilerParams(
            collective_id=0, has_side_effects=True, vmem_limit_bytes=62 << 20
        ),
        cost_estimate=pl.CostEstimate(flops=10**10, bytes_accessed=3 * 10**7, transcendentals=10**6),
        name="spectral",
    )(fields, cotangent, tw, th, tht, w_first, w_second, bias)


PAIR = 2
TILE_W = 128


def inverse_kernel(
    back_hbm,
    cot_hbm,
    twt_hbm,
    grad_ref,
    bias_ref,
    out_hbm,
    g1_ref,
    g2_ref,
    gb_ref,
    bs,
    back,
    buf,
    twt,
    back_sem,
    cot_sem,
    out_sem,
    twt_sem,
):
    xhi = lax.axis_index("lon")

    def load_back(g):
        return pltpu.make_async_copy(back_hbm.at[g], back.at[g], back_sem.at[g])

    def load_cot(g):
        rows = pl.ds(g * GH, GH)
        return pltpu.make_async_copy(cot_hbm.at[0, rows], buf.at[rows], cot_sem.at[g])

    def store(i):
        rows = pl.ds(i * PAIR, PAIR)
        return pltpu.make_async_copy(buf.at[rows], out_hbm.at[0, rows], out_sem.at[i])

    table = pltpu.make_async_copy(twt_hbm.at[xhi], twt, twt_sem.at[0])
    for g in range(NG):
        load_back(g).start()
        if g == 0:
            table.start()
        load_cot(g).start()

    scale = 1.0 / math.sqrt(SPEC_ROWS)
    row = lax.broadcasted_iota(jnp.int32, (LANES, BS), 0)
    col = lax.broadcasted_iota(jnp.int32, (LANES, BS), 1)
    for m in range(2):
        pick = (row == col + (xhi * 64 + m * BS)).astype(F32)

        def take(value):
            return scale * jnp.dot(
                value, pick, precision=lax.Precision.HIGHEST, preferred_element_type=F32
            )

        for r in range(2):
            g1_ref[m, r] = take(grad_ref[r].reshape(BS, LANES))
            g2_ref[m, r] = take(grad_ref[2 + r].reshape(BS, LANES))
        gb_ref[m] = take(bias_ref[...])[:2]
    table.wait()

    @pl.loop(0, NG)
    def _(g):
        load_back(g).wait()

        @pl.loop(0, NJ * ND)
        def _(jd):
            j, d = jd // ND, lax.rem(jd, ND)
            for ky in range(NY):
                rows = pl.ds(pl.multiple_of(jd * NY * SUB + ky * SUB, SUB), SUB)
                for ct in range(3):
                    bs[ct, rows, :] = back[g, j, d, ky, :, pl.ds(ct * 128, 128)].astype(F32)

        load_cot(g).wait()
        for hp in range(GH // PAIR):
            spec = jnp.concatenate(
                [
                    bs[ct, pl.ds(hp * PAIR + k, 2 * KW, stride=GH), :].astype(BF16)
                    for k in range(PAIR)
                    for ct in range(3)
                ],
                1,
            )
            for t in range(HALF // TILE_W):
                cols = pl.ds(t * TILE_W, TILE_W)
                part = dot(twt[cols, :], spec) * LON_NORM
                for k in range(PAIR):
                    h = g * GH + hp * PAIR + k
                    value = buf[h, cols].astype(F32) + part[:, k * CH : (k + 1) * CH]
                    buf[h, cols] = value.astype(BF16)
            store(g * (GH // PAIR) + hp).start()

    for i in range(ROWS // PAIR):
        store(i).wait()


def inverse_call(back, cotangent, twt, grads, bias):
    vm = pl.BlockSpec(memory_space=pltpu.VMEM)
    hbm = pl.BlockSpec(memory_space=pl.ANY)
    dma = pltpu.SemaphoreType.DMA
    return pl.pallas_call(
        inverse_kernel,
        out_shape=(
            jax.ShapeDtypeStruct((1, ROWS, HALF, CH), BF16),
            jax.ShapeDtypeStruct((2, 2, BS, BS), F32),
            jax.ShapeDtypeStruct((2, 2, BS, BS), F32),
            jax.ShapeDtypeStruct((2, 2, BS), F32),
        ),
        in_specs=[hbm, hbm, hbm, vm, vm],
        out_specs=(hbm, vm, vm, vm),
        scratch_shapes=[
            pltpu.VMEM((3, GH * 2 * KW, 128), F32),
            pltpu.VMEM((NG, NJ, ND, NY, SUB, CH), BF16),
            pltpu.VMEM((ROWS, HALF, CH), BF16),
            pltpu.VMEM((HALF, 2 * KW), BF16),
            dma((NG,)),
            dma((NG,)),
            dma((ROWS // PAIR,)),
            dma((1,)),
        ],
        compiler_params=pltpu.CompilerParams(vmem_limit_bytes=62 << 20),
        cost_estimate=pl.CostEstimate(
            flops=1400 * 10**6, bytes_accessed=18 * 10**6, transcendentals=0
        ),
        name="inverse",
    )(back, cotangent, twt, grads, bias)


def on_device(fields, cotangent, w_first, w_second, bias_first):
    tw, twt, th, tht = (jnp.asarray(table) for table in tables())
    back, grads, bias = spectral_call(
        fields, cotangent, tw, th, tht, w_first, w_second, bias_first
    )
    return inverse_call(back, cotangent, twt, grads, bias)


def solution(mesh):
    placed = (
        P("dp", "lat", "lon", None),
        P("dp", "lat", "lon", None),
        P("lon", None, None, None),
        P("lon", None, None, None),
        P("lon", None, None),
    )
    return jax.shard_map(
        on_device,
        mesh=mesh,
        in_specs=placed,
        out_specs=(
            P("dp", "lat", "lon", None),
            P("lon", None, None, None),
            P("lon", None, None, None),
            P("lon", None, None),
        ),
        check_vma=False,
    )
```

```python
import functools
import math

import jax
import jax.numpy as jnp
import numpy as np
from jax import lax
from jax.experimental import pallas as pl
from jax.experimental.pallas import tpu as pltpu
from jax.sharding import PartitionSpec as P

NLAT, NLON, KW, CH, BS, NBLK = 384, 768, 96, 384, 96, 4
HALF = NLON // 2
ROWS = 24
NG, GH = 3, 8
NJ = 3
ND = 8
NY = 4
NZ = 4
LANES = 256
SUB = 2 * GH
WAVES = 2 * KW // NJ
BLK = NG * SUB
QROWS = 4 * BLK
SPEC_ROWS = 4 * NLAT * KW

LON_NORM = 1.0 / math.sqrt(NLON)
LAT_NORM = 1.0 / math.sqrt(NLAT)
shrink_level = 0.05
gelu_coef = 0.044715
root = math.sqrt(2.0 / math.pi)

MESH = pl.DeviceIdType.MESH
F32, BF16 = jnp.float32, jnp.bfloat16


def cos_sin(phase_int, period):
    phase = phase_int.astype(np.float32) * np.float32(2.0 * math.pi / period)
    return np.cos(phase).astype(np.float32), np.sin(phase).astype(np.float32)


def tables():
    kk = np.arange(KW, dtype=np.int64)[:, None]
    ww = np.arange(NLON, dtype=np.int64)[None, :]
    cosine, sine = cos_sin(kk * ww % NLON, NLON)
    tw = np.stack([cosine, -sine], 1).reshape(2 * KW, 2, HALF).transpose(1, 0, 2)
    pp = np.arange(NLAT, dtype=np.int64)[:, None]
    hh = np.arange(NLAT, dtype=np.int64)[None, :]
    cosine, sine = cos_sin(pp * hh % NLAT, NLAT)
    th = np.stack([np.stack([cosine, sine], 0), np.stack([-sine, cosine], 0)], 0)
    th = th.transpose(0, 2, 1, 3).reshape(2 * NLAT, 2, NLAT // ROWS, NG, GH)
    th = th.transpose(0, 2, 3, 1, 4).reshape(2 * NLAT, 2 * NLAT)
    kind = jnp.bfloat16
    return (
        tw.astype(kind),
        np.ascontiguousarray(tw.transpose(0, 2, 1)).astype(kind),
        th.astype(kind),
        np.ascontiguousarray(th.T).astype(kind),
    )


def dot(a, b):
    return jnp.dot(a, b, preferred_element_type=F32)


def dot_nt(a, b):
    return lax.dot_general(a, b, (((1,), (1,)), ((), ())), preferred_element_type=F32)


def dot_tn(a, b):
    return lax.dot_general(a, b, (((0,), (0,)), ((), ())), preferred_element_type=F32)


def spectral_kernel(
    f_hbm,
    c_hbm,
    tw_hbm,
    th_hbm,
    tht_hbm,
    w1_ref,
    w2_ref,
    b1_ref,
    back_hbm,
    gout_ref,
    gbout_ref,
    w_all,
    b_all,
    wc1_ref,
    wc2_ref,
    bias_ref,
    gacc,
    gb_ref,
    gz,
    gzr,
    gy,
    gyr,
    gd,
    gdr,
    gyo,
    gzs,
    gzo,
    tw_ref,
    th_ref,
    tht_ref,
    fbuf,
    ps,
    xs,
    xr,
    ys,
    yr,
    yb,
    yrb,
    zbuf,
    hbuf,
    dobuf,
    dzbuf,
    slope,
    keep,
    dsbuf,
    ld_sem,
    table_sem,
    xl_sem,
    xsend,
    xrecv,
    yl_sem,
    ysend,
    yrecv,
    wl_sem,
    wsend,
    wrecv,
    gsend,
    grecv,
):
    lat = lax.axis_index("lat")
    xhi = lax.axis_index("lon")
    dp = lax.axis_index("dp")
    y = lat // 4
    me = xhi * 4 + lax.rem(lat, 4)

    def device(yy, d, zz=dp):
        return (zz, yy * 4 + lax.rem(d, 4), d // 4)

    def load(which, g):
        src = (f_hbm, c_hbm)[which]
        rows = pl.ds(g * GH, GH)
        return pltpu.make_async_copy(src.at[0, rows], fbuf.at[rows], ld_sem.at[which, g])

    def load_table(i):
        src = (tw_hbm.at[xhi], th_hbm, tht_hbm)[i]
        return pltpu.make_async_copy(src, (tw_ref, th_ref, tht_ref)[i], table_sem.at[i])

    load_table(0).start()
    for g in range(NG):
        load(0, g).start()

    barrier = pltpu.get_barrier_semaphore()
    for i in range(1, ND):
        d = lax.rem(me + i, ND)
        pl.semaphore_signal(barrier, inc=1, device_id=device(y, d), device_id_type=MESH)
    for i in range(1, NY):
        yy = lax.rem(y + i, NY)
        pl.semaphore_signal(barrier, inc=1, device_id=device(yy, me), device_id_type=MESH)
    for i in range(1, NZ):
        zz = lax.rem(dp + i, NZ)
        pl.semaphore_signal(barrier, inc=1, device_id=device(y, me, zz), device_id_type=MESH)
    pl.semaphore_wait(barrier, ND - 1 + NY - 1 + NZ - 1)

    def weight_refs(i):
        return ((w1_ref, w_all.at[0, xhi]), (w2_ref, w_all.at[1, xhi]), (b1_ref, b_all.at[xhi]))[i]

    def weight_copy(i):
        src, dst = weight_refs(i)
        return pltpu.make_async_remote_copy(
            src_ref=src,
            dst_ref=dst,
            send_sem=wsend.at[i],
            recv_sem=wrecv.at[i],
            device_id=device(y, lax.rem(me + 4, ND)),
            device_id_type=MESH,
        )

    def weight_local(i):
        src, dst = weight_refs(i)
        return pltpu.make_async_copy(src, dst, wl_sem.at[i])

    def weights_start():
        for i in range(3):
            weight_copy(i).start()
            weight_local(i).start()

    def weights_build():
        for i in range(3):
            weight_copy(i).wait()
            weight_local(i).wait()
        row = lax.broadcasted_iota(jnp.int32, (BS, CH), 0)
        col = lax.broadcasted_iota(jnp.int32, (BS, CH), 1)
        bias = jnp.zeros((2, CH), F32)
        for n in range(NBLK):
            spread = col == row + n * BS
            bias += jnp.dot(
                b_all[n // 2, n % 2],
                spread.astype(F32),
                precision=lax.Precision.HIGHEST,
                preferred_element_type=F32,
            )
            spread = spread.astype(F32).astype(BF16)
            top, low = pl.ds(n * BS, BS), pl.ds(CH + n * BS, BS)
            re, im = pl.ds(0, CH), pl.ds(CH, CH)
            for i, out in enumerate((wc1_ref, wc2_ref)):
                real = dot(w_all[i, n // 2, n % 2, 0], spread)
                imag = dot(w_all[i, n // 2, n % 2, 1], spread)
                out[top, re] = real.astype(BF16)
                out[low, im] = real.astype(BF16)
                out[top, im] = imag.astype(BF16)
                out[low, re] = (-imag).astype(BF16)
        for r in range(2):
            bias_ref[:, pl.ds(r * CH, CH)] = bias[r : r + 1]

    def x_refs(slot, d, frm):
        if slot >= 15:
            return xs.at[0, 0, d, slot - 15], xr.at[0, 0, frm, slot - 15]
        if slot < 6:
            return xs.at[slot // NJ, slot % NJ, d], xr.at[slot // NJ, slot % NJ, frm]
        j, g = (slot - 6) // NG, (slot - 6) % NG
        rows = pl.ds(pl.multiple_of(lax.rem(d, 4) * BLK + g * SUB, SUB), SUB)
        return yrb.at[j, :, rows], back_hbm.at[g, j, frm]

    def x_copy(slot, d, frm):
        src, dst = x_refs(slot, d, frm)
        return pltpu.make_async_remote_copy(
            src_ref=src,
            dst_ref=dst,
            send_sem=xsend.at[slot, d],
            recv_sem=xrecv.at[slot, frm],
            device_id=device(y, d),
            device_id_type=MESH,
        )

    def x_local(slot):
        src, dst = x_refs(slot, me, me)
        return pltpu.make_async_copy(src, dst, xl_sem.at[slot])

    def x_start(slot):
        @pl.loop(1, ND)
        def _(i):
            x_copy(slot, lax.rem(me + i, ND), me).start()

        x_local(slot).start()

    def x_wait_recv(slot):
        @pl.loop(1, ND)
        def _(i):
            frm = lax.rem(me + ND - i, ND)
            x_copy(slot, frm, frm).wait_recv()

        x_local(slot).wait()

    def x_wait_send(slot):
        @pl.loop(1, ND)
        def _(i):
            x_copy(slot, lax.rem(me + i, ND), me).wait_send()

    def y_refs(slot, yy, frm):
        if slot < 6:
            return ys.at[slot // NJ, slot % NJ, yy], yr.at[slot // NJ, slot % NJ, frm]
        return yb.at[slot - 6, yy], yrb.at[slot - 6, frm]

    def y_copy(slot, yy, frm):
        src, dst = y_refs(slot, yy, frm)
        return pltpu.make_async_remote_copy(
            src_ref=src,
            dst_ref=dst,
            send_sem=ysend.at[slot, yy],
            recv_sem=yrecv.at[slot, frm],
            device_id=device(yy, me),
            device_id_type=MESH,
        )

    def y_local(slot):
        src, dst = y_refs(slot, y, y)
        return pltpu.make_async_copy(src, dst, yl_sem.at[slot])

    def y_start(slot):
        @pl.loop(1, NY)
        def _(i):
            y_copy(slot, lax.rem(y + i, NY), y).start()

        y_local(slot).start()

    def y_wait_recv(slot):
        @pl.loop(1, NY)
        def _(i):
            frm = lax.rem(y + NY - i, NY)
            y_copy(slot, frm, frm).wait_recv()

        y_local(slot).wait()

    def y_wait_send(slot):
        @pl.loop(1, NY)
        def _(i):
            y_copy(slot, lax.rem(y + i, NY), y).wait_send()

    def lon_group(which, j, g):
        left = tw_ref[pl.ds(j * WAVES, WAVES), :]
        for h in range(GH):
            part = dot(left, fbuf[g * GH + h])
            for ct in range(3):
                ps[ct, pl.ds(h * WAVES, WAVES), :] = part[:, ct * 128 : (ct + 1) * 128]

        @pl.loop(0, ND)
        def _(d):
            for ky in range(NY):
                base = (d * NY + ky) * 2
                for ct in range(3):
                    tile = jnp.concatenate(
                        [ps[ct, pl.ds(base + r, GH, stride=WAVES), :] for r in range(2)], 0
                    )
                    xs[which, j, d, g, ky, :, pl.ds(ct * 128, 128)] = (tile * LON_NORM).astype(BF16)

    def lon_chunk(which, j):
        @pl.loop(0, NG)
        def _(g):
            lon_group(which, j, g)

    def x_sum(which, j):
        @pl.loop(0, 4)
        def _(s):
            for g in range(NG):
                for ky in range(NY):
                    both = xr[which, j, s, g, ky].astype(F32) + xr[which, j, s + 4, g, ky].astype(F32)
                    rows = pl.ds(pl.multiple_of(s * BLK + g * SUB, SUB), SUB)
                    ys[which, j, ky, rows, :] = both.astype(BF16)

    def x_to_y(which, j):
        for slot in (15, 16, 17) if which == j == 0 else (NJ * which + j,):
            x_wait_recv(slot)
        if which == 0:
            x_start(NJ + j)
        x_sum(which, j)
        y_start(NJ * which + j)

    TILE = 192

    def forward(j):
        @pl.loop(0, 2)
        def _(t):
            rows = pl.ds(pl.multiple_of(t * TILE, TILE), TILE)
            for q in range(2):
                trows = pl.ds(pl.multiple_of(q * NLAT + t * TILE, TILE), TILE)
                zbuf[j, rows, pl.ds(q * CH, CH)] = (
                    dot(th_ref[trows, :], yr[0, j].reshape(2 * NLAT, CH)) * LAT_NORM
                ).astype(BF16)
            o1 = dot(zbuf[j, rows, :], wc1_ref[...]) + bias_ref[...]
            square = o1 * o1
            tangent = jnp.tanh(root * (o1 + gelu_coef * o1 * square))
            hbuf[j, rows, :] = (0.5 * o1 * (1.0 + tangent)).astype(BF16)
            slope[j, rows, :] = 0.5 * (1.0 + tangent) + 0.5 * o1 * (
                1.0 - tangent * tangent
            ) * root * (1.0 + 3.0 * gelu_coef * square)
            o2 = dot(hbuf[j, rows, :], wc2_ref[...])
            square = o2 * o2
            keep[j, rows, :] = square / (square + shrink_level * shrink_level)

    def backward(j):
        wave = (j * ND + me) * NY + y
        doubling = jnp.where(wave == 0, 1.0, 2.0).astype(F32) * LAT_NORM

        @pl.loop(0, 2)
        def _(t):
            rows = pl.ds(pl.multiple_of(t * TILE, TILE), TILE)
            for q in range(2):
                trows = pl.ds(pl.multiple_of(q * NLAT + t * TILE, TILE), TILE)
                cols = pl.ds(q * CH, CH)
                gm = dot(th_ref[trows, :], yr[1, j].reshape(2 * NLAT, CH)) * doubling
                dobuf[rows, cols] = (keep[j, rows, cols] * gm).astype(BF16)
            dh = dot_nt(dobuf[rows, :], wc2_ref[...])
            dz = (slope[j, rows, :] * dh).astype(BF16)
            dzbuf[rows, :] = dz
            gb_ref[...] += jnp.sum(dz.astype(F32), 0, keepdims=True)
            ds = dot_nt(dz, wc1_ref[...]).astype(BF16)
            for q in range(2):
                trows = pl.ds(pl.multiple_of(q * NLAT + t * TILE, TILE), TILE)
                dsbuf[trows, :] = ds[:, q * CH : (q + 1) * CH]

    def back(j):
        @pl.loop(0, NY)
        def _(yy):
            rows = pl.ds(pl.multiple_of(yy * QROWS, QROWS), QROWS)
            yb[j, yy] = (dot(tht_ref[rows, :], dsbuf[...]) * LAT_NORM).astype(BF16)

    def weight_grads(j):
        re, im = pl.ds(0, CH), pl.ds(CH, CH)
        for i, (zz, dd) in enumerate(((zbuf, dzbuf), (hbuf, dobuf))):
            gacc[2 * i] += dot_tn(zz[j, :, re], dd[:, re]) + dot_tn(zz[j, :, im], dd[:, im])
            gacc[2 * i + 1] += dot_tn(zz[j, :, re], dd[:, im]) - dot_tn(zz[j, :, im], dd[:, re])

    def grad_copy(stage, to, frm):
        src, dst, target = (
            lambda: (gz.at[to], gzr.at[frm], device(y, me, to)),
            lambda: (gy.at[to], gyr.at[frm], device(to, me)),
            lambda: (gd, gdr.at[frm], device(y, to)),
            lambda: (gd.at[pl.ds(0, BS // NY), lanes], gyo.at[frm], device(to, me)),
            lambda: (gzs, gzo.at[frm], device(y, me, to)),
        )[stage]()
        return pltpu.make_async_remote_copy(
            src_ref=src,
            dst_ref=dst,
            send_sem=gsend.at[stage, to],
            recv_sem=grecv.at[stage, frm],
            device_id=target,
            device_id_type=MESH,
        )

    lanes = pl.ds(pl.multiple_of(xhi * 128, 128), LANES)
    stage_size = (NZ, NY, ND, NY, NZ)
    stage_place = (dp, y, me, y, dp)

    def grad_start(stage):
        here, size = stage_place[stage], stage_size[stage]

        @pl.loop(1, size)
        def _(i):
            grad_copy(stage, lax.rem(here + i, size), here).start()

    def grad_wait(stage):
        here, size = stage_place[stage], stage_size[stage]

        @pl.loop(1, size)
        def _(i):
            frm = lax.rem(here + size - i, size)
            grad_copy(stage, frm, frm).wait_recv()

        @pl.loop(1, size)
        def _(i):
            grad_copy(stage, lax.rem(here + i, size), here).wait_send()

    def grad_begin():
        lane = lax.broadcasted_iota(jnp.int32, (BS, CH), 1)
        line = lax.broadcasted_iota(jnp.int32, (SUB, CH), 0)
        both = [jnp.broadcast_to(gb_ref[:, pl.ds(r * CH, CH)], (SUB, CH)) for r in range(2)]
        sums = jnp.where(line == 0, both[0], jnp.where(line == 1, both[1], 0.0))
        for i in range(NZ):
            part = gacc[i, pl.ds(0, BS), :]
            for n in range(1, NBLK):
                part = jnp.where(lane >= n * BS, gacc[i, pl.ds(n * BS, BS), :], part)
            gz[i, pl.ds(0, BS), :] = part.astype(BF16)
            gz[i, pl.ds(BS, SUB), :] = sums.astype(BF16)
        gzr[dp] = gz[dp]
        grad_start(0)

    def grad_finish(before_exchange, after_exchange_starts):
        part = BS // NY
        grad_wait(0)
        total = gzr[0].astype(F32)
        for i in range(1, NZ):
            total += gzr[i].astype(F32)
        for i in range(NY):
            gy[i, pl.ds(0, part), :] = total[i * part : (i + 1) * part]
            gy[i, pl.ds(part, 8), :] = total[BS : BS + 8]
        gyr[y] = gy[y]
        grad_start(1)
        before_exchange()
        grad_wait(1)
        gd[...] = gyr[0] + gyr[1] + gyr[2] + gyr[3]
        gdr[me] = gd[...]
        grad_start(2)
        after_exchange_starts()
        grad_wait(2)
        total = gdr[0]
        for i in range(1, ND):
            total += gdr[i]
        gd[...] = total
        gbout_ref[...] = gd[pl.ds(part, 8), lanes]
        gyo[y] = gd[pl.ds(0, part), lanes]
        grad_start(3)
        grad_wait(3)
        gzs[...] = gyo[...].reshape(BS, LANES).astype(BF16)
        gzo[dp] = gzs[...]
        grad_start(4)
        grad_wait(4)
        gout_ref[...] = gzo[...].astype(F32).reshape(NZ, NY, part, LANES)

    weights_start()
    load_table(0).wait()
    for g in range(NG):
        load(0, g).wait()
        lon_group(0, 0, g)
        x_start(15 + g)
    for i in range(1, 3):
        load_table(i).start()
    for j in range(1, NJ):
        lon_chunk(0, j)
        x_start(j)
    for g in range(NG):
        load(1, g).start()
    gacc[...] = jnp.zeros_like(gacc)
    gb_ref[...] = jnp.zeros_like(gb_ref)
    weights_build()
    for g in range(NG):
        load(1, g).wait()
    lon_chunk(1, 0)
    x_to_y(0, 0)
    for j in range(1, NJ):
        lon_chunk(1, j)
    x_to_y(0, 1)
    for i in range(1, 3):
        load_table(i).wait()
    for j in range(2):
        y_wait_recv(j)
        forward(j)
    x_to_y(0, 2)
    y_wait_recv(2)
    forward(2)
    x_to_y(1, 0)
    y_wait_recv(3)
    backward(0)
    back(0)
    x_to_y(1, 1)
    weight_grads(0)
    y_wait_recv(4)
    y_start(6)
    backward(1)
    back(1)
    y_wait_recv(6)
    x_start(6)
    x_to_y(1, 2)
    x_start(7)
    x_start(8)
    weight_grads(1)
    y_wait_recv(5)
    y_start(7)
    backward(2)
    weight_grads(2)
    grad_begin()
    back(2)
    y_wait_recv(7)
    x_start(9)
    x_start(10)
    y_start(8)

    def last_return():
        y_wait_recv(8)
        for g in range(NG):
            x_start(12 + g)

    grad_finish(lambda: x_start(11), last_return)
    for slot in range(6, 15):
        x_wait_recv(slot)
    for slot in range(1, 18):
        x_wait_send(slot)
    for slot in range(9):
        y_wait_send(slot)


def spectral_call(fields, cotangent, tw, th, tht, w_first, w_second, bias):
    vm = pl.BlockSpec(memory_space=pltpu.VMEM)
    hbm = pl.BlockSpec(memory_space=pl.ANY)
    dma = pltpu.SemaphoreType.DMA
    return pl.pallas_call(
        spectral_kernel,
        out_shape=(
            jax.ShapeDtypeStruct((NG, NJ, ND, NY, SUB, CH), BF16),
            jax.ShapeDtypeStruct((NZ, NY, BS // NY, LANES), F32),
            jax.ShapeDtypeStruct((8, LANES), F32),
        ),
        in_specs=[hbm] * 5 + [vm] * 3,
        out_specs=(hbm, vm, vm),
        scratch_shapes=[
            pltpu.VMEM((2, 2, 2, 2, BS, BS), BF16),
            pltpu.VMEM((2, 2, 2, BS), F32),
            pltpu.VMEM((2 * CH, 2 * CH), BF16),
            pltpu.VMEM((2 * CH, 2 * CH), BF16),
            pltpu.VMEM((1, 2 * CH), F32),
            pltpu.VMEM((4, CH, CH), F32),
            pltpu.VMEM((1, 2 * CH), F32),
            pltpu.VMEM((NZ, BS + SUB, CH), BF16),
            pltpu.VMEM((NZ, BS + SUB, CH), BF16),
            pltpu.VMEM((NY, BS // NY + 8, CH), F32),
            pltpu.VMEM((NY, BS // NY + 8, CH), F32),
            pltpu.VMEM((BS // NY + 8, CH), F32),
            pltpu.VMEM((ND, BS // NY + 8, CH), F32),
            pltpu.VMEM((NY, BS // NY, LANES), F32),
            pltpu.VMEM((BS, LANES), BF16),
            pltpu.VMEM((NZ, BS, LANES), BF16),
            pltpu.VMEM((2 * KW, HALF), BF16),
            pltpu.VMEM((2 * NLAT, 2 * NLAT), BF16),
            pltpu.VMEM((2 * NLAT, 2 * NLAT), BF16),
            pltpu.VMEM((ROWS, HALF, CH), BF16),
            pltpu.VMEM((3, GH * WAVES, 128), F32),
            pltpu.VMEM((2, NJ, ND, NG, NY, SUB, CH), BF16),
            pltpu.VMEM((2, NJ, ND, NG, NY, SUB, CH), BF16),
            pltpu.VMEM((2, NJ, NY, QROWS, CH), BF16),
            pltpu.VMEM((2, NJ, NY, QROWS, CH), BF16),
            pltpu.VMEM((NJ, NY, QROWS, CH), BF16),
            pltpu.VMEM((NJ, NY, QROWS, CH), BF16),
            pltpu.VMEM((NJ, NLAT, 2 * CH), BF16),
            pltpu.VMEM((NJ, NLAT, 2 * CH), BF16),
            pltpu.VMEM((NLAT, 2 * CH), BF16),
            pltpu.VMEM((NLAT, 2 * CH), BF16),
            pltpu.VMEM((NJ, NLAT, 2 * CH), F32),
            pltpu.VMEM((NJ, NLAT, 2 * CH), F32),
            pltpu.VMEM((2 * NLAT, CH), BF16),
            dma((2, NG)),
            dma((3,)),
            dma((18,)),
            dma((18, ND)),
            dma((18, ND)),
            dma((9,)),
            dma((9, NY)),
            dma((9, NY)),
            dma((3,)),
            dma((3,)),
            dma((3,)),
            dma((5, ND)),
            dma((5, ND)),
        ],
        compiler_params=pltpu.CompilerParams(
            collective_id=0, has_side_effects=True, vmem_limit_bytes=62 << 20
        ),
        cost_estimate=pl.CostEstimate(flops=10**10, bytes_accessed=3 * 10**7, transcendentals=10**6),
        name="spectral",
    )(fields, cotangent, tw, th, tht, w_first, w_second, bias)


PAIR = 2
TILE_W = 128


def inverse_kernel(
    back_hbm,
    cot_hbm,
    twt_hbm,
    grad_ref,
    bias_ref,
    out_hbm,
    g1_ref,
    g2_ref,
    gb_ref,
    bs,
    back,
    buf,
    twt,
    back_sem,
    cot_sem,
    out_sem,
    twt_sem,
):
    xhi = lax.axis_index("lon")

    def load_back(g):
        return pltpu.make_async_copy(back_hbm.at[g], back.at[g], back_sem.at[g])

    def load_cot(g):
        rows = pl.ds(g * GH, GH)
        return pltpu.make_async_copy(cot_hbm.at[0, rows], buf.at[rows], cot_sem.at[g])

    def store(i):
        rows = pl.ds(i * PAIR, PAIR)
        return pltpu.make_async_copy(buf.at[rows], out_hbm.at[0, rows], out_sem.at[i])

    table = pltpu.make_async_copy(twt_hbm.at[xhi], twt, twt_sem.at[0])
    for g in range(NG):
        load_back(g).start()
        if g == 0:
            table.start()
        load_cot(g).start()

    scale = 1.0 / math.sqrt(SPEC_ROWS)
    row = lax.broadcasted_iota(jnp.int32, (LANES, BS), 0)
    col = lax.broadcasted_iota(jnp.int32, (LANES, BS), 1)
    for m in range(2):
        pick = (row == col + (xhi * 64 + m * BS)).astype(F32)

        def take(value):
            return scale * jnp.dot(
                value, pick, precision=lax.Precision.HIGHEST, preferred_element_type=F32
            )

        for r in range(2):
            g1_ref[m, r] = take(grad_ref[r].reshape(BS, LANES))
            g2_ref[m, r] = take(grad_ref[2 + r].reshape(BS, LANES))
        gb_ref[m] = take(bias_ref[...])[:2]
    table.wait()

    @pl.loop(0, NG)
    def _(g):
        load_back(g).wait()

        @pl.loop(0, NJ * ND)
        def _(jd):
            j, d = jd // ND, lax.rem(jd, ND)
            for ky in range(NY):
                rows = pl.ds(pl.multiple_of(jd * NY * SUB + ky * SUB, SUB), SUB)
                for ct in range(3):
                    bs[ct, rows, :] = back[g, j, d, ky, :, pl.ds(ct * 128, 128)].astype(F32)

        load_cot(g).wait()
        for hp in range(GH // PAIR):
            spec = jnp.concatenate(
                [
                    bs[ct, pl.ds(hp * PAIR + k, 2 * KW, stride=GH), :].astype(BF16)
                    for k in range(PAIR)
                    for ct in range(3)
                ],
                1,
            )
            for t in range(HALF // TILE_W):
                cols = pl.ds(t * TILE_W, TILE_W)
                part = dot(twt[cols, :], spec) * LON_NORM
                for k in range(PAIR):
                    h = g * GH + hp * PAIR + k
                    value = buf[h, cols].astype(F32) + part[:, k * CH : (k + 1) * CH]
                    buf[h, cols] = value.astype(BF16)
            store(g * (GH // PAIR) + hp).start()

    for i in range(ROWS // PAIR):
        store(i).wait()


def inverse_call(back, cotangent, twt, grads, bias):
    vm = pl.BlockSpec(memory_space=pltpu.VMEM)
    hbm = pl.BlockSpec(memory_space=pl.ANY)
    dma = pltpu.SemaphoreType.DMA
    return pl.pallas_call(
        inverse_kernel,
        out_shape=(
            jax.ShapeDtypeStruct((1, ROWS, HALF, CH), BF16),
            jax.ShapeDtypeStruct((2, 2, BS, BS), F32),
            jax.ShapeDtypeStruct((2, 2, BS, BS), F32),
            jax.ShapeDtypeStruct((2, 2, BS), F32),
        ),
        in_specs=[hbm, hbm, hbm, vm, vm],
        out_specs=(hbm, vm, vm, vm),
        scratch_shapes=[
            pltpu.VMEM((3, GH * 2 * KW, 128), F32),
            pltpu.VMEM((NG, NJ, ND, NY, SUB, CH), BF16),
            pltpu.VMEM((ROWS, HALF, CH), BF16),
            pltpu.VMEM((HALF, 2 * KW), BF16),
            dma((NG,)),
            dma((NG,)),
            dma((ROWS // PAIR,)),
            dma((1,)),
        ],
        compiler_params=pltpu.CompilerParams(vmem_limit_bytes=62 << 20),
        cost_estimate=pl.CostEstimate(
            flops=1400 * 10**6, bytes_accessed=18 * 10**6, transcendentals=0
        ),
        name="inverse",
    )(back, cotangent, twt, grads, bias)


def on_device(fields, cotangent, w_first, w_second, bias_first):
    tw, twt, th, tht = (jnp.asarray(table) for table in tables())
    back, grads, bias = spectral_call(
        fields, cotangent, tw, th, tht, w_first, w_second, bias_first
    )
    return inverse_call(back, cotangent, twt, grads, bias)


def solution(mesh):
    placed = (
        P("dp", "lat", "lon", None),
        P("dp", "lat", "lon", None),
        P("lon", None, None, None),
        P("lon", None, None, None),
        P("lon", None, None),
    )
    return jax.shard_map(
        on_device,
        mesh=mesh,
        in_specs=placed,
        out_specs=(
            P("dp", "lat", "lon", None),
            P("lon", None, None, None),
            P("lon", None, None, None),
            P("lon", None, None),
        ),
        check_vma=False,
    )
```

```python
import functools
import math

import jax
import jax.numpy as jnp
import numpy as np
from jax import lax
from jax.experimental import pallas as pl
from jax.experimental.pallas import tpu as pltpu
from jax.sharding import PartitionSpec as P

NLAT, NLON, KW, CH, BS, NBLK = 384, 768, 96, 384, 96, 4
HALF = NLON // 2
ROWS = 24
NG, GH = 3, 8
NJ = 3
ND = 8
NY = 4
NZ = 4
LANES = 256
SUB = 2 * GH
WAVES = 2 * KW // NJ
BLK = NG * SUB
QROWS = 4 * BLK
SPEC_ROWS = 4 * NLAT * KW

LON_NORM = 1.0 / math.sqrt(NLON)
LAT_NORM = 1.0 / math.sqrt(NLAT)
shrink_level = 0.05
gelu_coef = 0.044715
root = math.sqrt(2.0 / math.pi)

MESH = pl.DeviceIdType.MESH
F32, BF16 = jnp.float32, jnp.bfloat16


def cos_sin(phase_int, period):
    phase = phase_int.astype(np.float32) * np.float32(2.0 * math.pi / period)
    return np.cos(phase).astype(np.float32), np.sin(phase).astype(np.float32)


def tables():
    kk = np.arange(KW, dtype=np.int64)[:, None]
    ww = np.arange(NLON, dtype=np.int64)[None, :]
    cosine, sine = cos_sin(kk * ww % NLON, NLON)
    tw = np.stack([cosine, -sine], 1).reshape(2 * KW, 2, HALF).transpose(1, 0, 2)
    pp = np.arange(NLAT, dtype=np.int64)[:, None]
    hh = np.arange(NLAT, dtype=np.int64)[None, :]
    cosine, sine = cos_sin(pp * hh % NLAT, NLAT)
    th = np.stack([np.stack([cosine, sine], 0), np.stack([-sine, cosine], 0)], 0)
    th = th.transpose(0, 2, 1, 3).reshape(2 * NLAT, 2, NLAT // ROWS, NG, GH)
    th = th.transpose(0, 2, 3, 1, 4).reshape(2 * NLAT, 2 * NLAT)
    kind = jnp.bfloat16
    return (
        tw.astype(kind),
        np.ascontiguousarray(tw.transpose(0, 2, 1)).astype(kind),
        th.astype(kind),
        np.ascontiguousarray(th.T).astype(kind),
    )


def dot(a, b):
    return jnp.dot(a, b, preferred_element_type=F32)


def dot_nt(a, b):
    return lax.dot_general(a, b, (((1,), (1,)), ((), ())), preferred_element_type=F32)


def dot_tn(a, b):
    return lax.dot_general(a, b, (((0,), (0,)), ((), ())), preferred_element_type=F32)


def spectral_kernel(
    f_hbm,
    c_hbm,
    tw_hbm,
    th_hbm,
    tht_hbm,
    w1_ref,
    w2_ref,
    b1_ref,
    back_hbm,
    gout_ref,
    gbout_ref,
    w_all,
    b_all,
    wc1_ref,
    wc2_ref,
    bias_ref,
    gacc,
    gb_ref,
    gz,
    gzr,
    gy,
    gyr,
    gd,
    gdr,
    gyo,
    gzs,
    gzo,
    tw_ref,
    th_ref,
    tht_ref,
    fbuf,
    ps,
    xs,
    xr,
    ys,
    yr,
    yb,
    yrb,
    zbuf,
    hbuf,
    dobuf,
    dzbuf,
    slope,
    keep,
    dsbuf,
    ld_sem,
    table_sem,
    xl_sem,
    xsend,
    xrecv,
    yl_sem,
    ysend,
    yrecv,
    wl_sem,
    wsend,
    wrecv,
    gsend,
    grecv,
):
    lat = lax.axis_index("lat")
    xhi = lax.axis_index("lon")
    dp = lax.axis_index("dp")
    y = lat // 4
    me = xhi * 4 + lax.rem(lat, 4)

    def device(yy, d, zz=dp):
        return (zz, yy * 4 + lax.rem(d, 4), d // 4)

    def load(which, g):
        src = (f_hbm, c_hbm)[which]
        rows = pl.ds(g * GH, GH)
        return pltpu.make_async_copy(src.at[0, rows], fbuf.at[rows], ld_sem.at[which, g])

    def load_table(i):
        src = (tw_hbm.at[xhi], th_hbm, tht_hbm)[i]
        return pltpu.make_async_copy(src, (tw_ref, th_ref, tht_ref)[i], table_sem.at[i])

    load_table(0).start()
    for g in range(NG):
        load(0, g).start()

    barrier = pltpu.get_barrier_semaphore()
    for i in range(1, ND):
        d = lax.rem(me + i, ND)
        pl.semaphore_signal(barrier, inc=1, device_id=device(y, d), device_id_type=MESH)
    for i in range(1, NY):
        yy = lax.rem(y + i, NY)
        pl.semaphore_signal(barrier, inc=1, device_id=device(yy, me), device_id_type=MESH)
    for i in range(1, NZ):
        zz = lax.rem(dp + i, NZ)
        pl.semaphore_signal(barrier, inc=1, device_id=device(y, me, zz), device_id_type=MESH)
    pl.semaphore_wait(barrier, ND - 1 + NY - 1 + NZ - 1)

    def weight_refs(i):
        return ((w1_ref, w_all.at[0, xhi]), (w2_ref, w_all.at[1, xhi]), (b1_ref, b_all.at[xhi]))[i]

    def weight_copy(i):
        src, dst = weight_refs(i)
        return pltpu.make_async_remote_copy(
            src_ref=src,
            dst_ref=dst,
            send_sem=wsend.at[i],
            recv_sem=wrecv.at[i],
            device_id=device(y, lax.rem(me + 4, ND)),
            device_id_type=MESH,
        )

    def weight_local(i):
        src, dst = weight_refs(i)
        return pltpu.make_async_copy(src, dst, wl_sem.at[i])

    def weights_start():
        for i in range(3):
            weight_copy(i).start()
            weight_local(i).start()

    def weights_build():
        for i in range(3):
            weight_copy(i).wait()
            weight_local(i).wait()
        row = lax.broadcasted_iota(jnp.int32, (BS, CH), 0)
        col = lax.broadcasted_iota(jnp.int32, (BS, CH), 1)
        bias = jnp.zeros((2, CH), F32)
        for n in range(NBLK):
            spread = col == row + n * BS
            bias += jnp.dot(
                b_all[n // 2, n % 2],
                spread.astype(F32),
                precision=lax.Precision.HIGHEST,
                preferred_element_type=F32,
            )
            spread = spread.astype(F32).astype(BF16)
            top, low = pl.ds(n * BS, BS), pl.ds(CH + n * BS, BS)
            re, im = pl.ds(0, CH), pl.ds(CH, CH)
            for i, out in enumerate((wc1_ref, wc2_ref)):
                real = dot(w_all[i, n // 2, n % 2, 0], spread)
                imag = dot(w_all[i, n // 2, n % 2, 1], spread)
                out[top, re] = real.astype(BF16)
                out[low, im] = real.astype(BF16)
                out[top, im] = imag.astype(BF16)
                out[low, re] = (-imag).astype(BF16)
        for r in range(2):
            bias_ref[:, pl.ds(r * CH, CH)] = bias[r : r + 1]

    def x_refs(slot, d, frm):
        if slot >= 15:
            return xs.at[0, 0, d, slot - 15], xr.at[0, 0, frm, slot - 15]
        if slot < 6:
            return xs.at[slot // NJ, slot % NJ, d], xr.at[slot // NJ, slot % NJ, frm]
        j, g = (slot - 6) // NG, (slot - 6) % NG
        rows = pl.ds(pl.multiple_of(lax.rem(d, 4) * BLK + g * SUB, SUB), SUB)
        return yrb.at[j, :, rows], back_hbm.at[g, j, frm]

    def x_copy(slot, d, frm):
        src, dst = x_refs(slot, d, frm)
        return pltpu.make_async_remote_copy(
            src_ref=src,
            dst_ref=dst,
            send_sem=xsend.at[slot, d],
            recv_sem=xrecv.at[slot, frm],
            device_id=device(y, d),
            device_id_type=MESH,
        )

    def x_local(slot):
        src, dst = x_refs(slot, me, me)
        return pltpu.make_async_copy(src, dst, xl_sem.at[slot])

    def x_start(slot):
        @pl.loop(1, ND)
        def _(i):
            x_copy(slot, lax.rem(me + i, ND), me).start()

        x_local(slot).start()

    def x_wait_recv(slot):
        @pl.loop(1, ND)
        def _(i):
            frm = lax.rem(me + ND - i, ND)
            x_copy(slot, frm, frm).wait_recv()

        x_local(slot).wait()

    def x_wait_send(slot):
        @pl.loop(1, ND)
        def _(i):
            x_copy(slot, lax.rem(me + i, ND), me).wait_send()

    def y_refs(slot, yy, frm):
        if slot < 6:
            return ys.at[slot // NJ, slot % NJ, yy], yr.at[slot // NJ, slot % NJ, frm]
        return yb.at[slot - 6, yy], yrb.at[slot - 6, frm]

    def y_copy(slot, yy, frm):
        src, dst = y_refs(slot, yy, frm)
        return pltpu.make_async_remote_copy(
            src_ref=src,
            dst_ref=dst,
            send_sem=ysend.at[slot, yy],
            recv_sem=yrecv.at[slot, frm],
            device_id=device(yy, me),
            device_id_type=MESH,
        )

    def y_local(slot):
        src, dst = y_refs(slot, y, y)
        return pltpu.make_async_copy(src, dst, yl_sem.at[slot])

    def y_start(slot):
        @pl.loop(1, NY)
        def _(i):
            y_copy(slot, lax.rem(y + i, NY), y).start()

        y_local(slot).start()

    def y_wait_recv(slot):
        @pl.loop(1, NY)
        def _(i):
            frm = lax.rem(y + NY - i, NY)
            y_copy(slot, frm, frm).wait_recv()

        y_local(slot).wait()

    def y_wait_send(slot):
        @pl.loop(1, NY)
        def _(i):
            y_copy(slot, lax.rem(y + i, NY), y).wait_send()

    def lon_group(which, j, g):
        left = tw_ref[pl.ds(j * WAVES, WAVES), :]
        for h in range(GH):
            part = dot(left, fbuf[g * GH + h])
            for ct in range(3):
                ps[ct, pl.ds(h * WAVES, WAVES), :] = part[:, ct * 128 : (ct + 1) * 128]

        @pl.loop(0, ND)
        def _(d):
            for ky in range(NY):
                base = (d * NY + ky) * 2
                for ct in range(3):
                    tile = jnp.concatenate(
                        [ps[ct, pl.ds(base + r, GH, stride=WAVES), :] for r in range(2)], 0
                    )
                    xs[which, j, d, g, ky, :, pl.ds(ct * 128, 128)] = (tile * LON_NORM).astype(BF16)

    def lon_chunk(which, j):
        @pl.loop(0, NG)
        def _(g):
            lon_group(which, j, g)

    def x_sum(which, j):
        @pl.loop(0, 4)
        def _(s):
            for g in range(NG):
                for ky in range(NY):
                    both = xr[which, j, s, g, ky].astype(F32) + xr[which, j, s + 4, g, ky].astype(F32)
                    rows = pl.ds(pl.multiple_of(s * BLK + g * SUB, SUB), SUB)
                    ys[which, j, ky, rows, :] = both.astype(BF16)

    def x_to_y(which, j):
        for slot in (15, 16, 17) if which == j == 0 else (NJ * which + j,):
            x_wait_recv(slot)
        if which == 0:
            x_start(NJ + j)
        x_sum(which, j)
        y_start(NJ * which + j)

    TILE = 192

    def forward(j):
        @pl.loop(0, 2)
        def _(t):
            rows = pl.ds(pl.multiple_of(t * TILE, TILE), TILE)
            for q in range(2):
                trows = pl.ds(pl.multiple_of(q * NLAT + t * TILE, TILE), TILE)
                zbuf[j, rows, pl.ds(q * CH, CH)] = (
                    dot(th_ref[trows, :], yr[0, j].reshape(2 * NLAT, CH)) * LAT_NORM
                ).astype(BF16)
            o1 = dot(zbuf[j, rows, :], wc1_ref[...]) + bias_ref[...]
            square = o1 * o1
            tangent = jnp.tanh(root * (o1 + gelu_coef * o1 * square))
            hbuf[j, rows, :] = (0.5 * o1 * (1.0 + tangent)).astype(BF16)
            slope[j, rows, :] = 0.5 * (1.0 + tangent) + 0.5 * o1 * (
                1.0 - tangent * tangent
            ) * root * (1.0 + 3.0 * gelu_coef * square)
            o2 = dot(hbuf[j, rows, :], wc2_ref[...])
            square = o2 * o2
            keep[j, rows, :] = square / (square + shrink_level * shrink_level)

    def backward(j):
        wave = (j * ND + me) * NY + y
        doubling = jnp.where(wave == 0, 1.0, 2.0).astype(F32) * LAT_NORM

        @pl.loop(0, 2)
        def _(t):
            rows = pl.ds(pl.multiple_of(t * TILE, TILE), TILE)
            for q in range(2):
                trows = pl.ds(pl.multiple_of(q * NLAT + t * TILE, TILE), TILE)
                cols = pl.ds(q * CH, CH)
                gm = dot(th_ref[trows, :], yr[1, j].reshape(2 * NLAT, CH)) * doubling
                dobuf[rows, cols] = (keep[j, rows, cols] * gm).astype(BF16)
            dh = dot_nt(dobuf[rows, :], wc2_ref[...])
            dz = (slope[j, rows, :] * dh).astype(BF16)
            dzbuf[rows, :] = dz
            gb_ref[...] += jnp.sum(dz.astype(F32), 0, keepdims=True)
            ds = dot_nt(dz, wc1_ref[...]).astype(BF16)
            for q in range(2):
                trows = pl.ds(pl.multiple_of(q * NLAT + t * TILE, TILE), TILE)
                dsbuf[trows, :] = ds[:, q * CH : (q + 1) * CH]

    def back(j):
        @pl.loop(0, NY)
        def _(yy):
            rows = pl.ds(pl.multiple_of(yy * QROWS, QROWS), QROWS)
            yb[j, yy] = (dot(tht_ref[rows, :], dsbuf[...]) * LAT_NORM).astype(BF16)

    def weight_grads(j):
        re, im = pl.ds(0, CH), pl.ds(CH, CH)
        for i, (zz, dd) in enumerate(((zbuf, dzbuf), (hbuf, dobuf))):
            gacc[2 * i] += dot_tn(zz[j, :, re], dd[:, re]) + dot_tn(zz[j, :, im], dd[:, im])
            gacc[2 * i + 1] += dot_tn(zz[j, :, re], dd[:, im]) - dot_tn(zz[j, :, im], dd[:, re])

    def grad_copy(stage, to, frm):
        src, dst, target = (
            lambda: (gz.at[to], gzr.at[frm], device(y, me, to)),
            lambda: (gy.at[to], gyr.at[frm], device(to, me)),
            lambda: (gd, gdr.at[frm], device(y, to)),
            lambda: (gd.at[pl.ds(0, BS // NY), lanes], gyo.at[frm], device(to, me)),
            lambda: (gzs, gzo.at[frm], device(y, me, to)),
        )[stage]()
        return pltpu.make_async_remote_copy(
            src_ref=src,
            dst_ref=dst,
            send_sem=gsend.at[stage, to],
            recv_sem=grecv.at[stage, frm],
            device_id=target,
            device_id_type=MESH,
        )

    lanes = pl.ds(pl.multiple_of(xhi * 128, 128), LANES)
    stage_size = (NZ, NY, ND, NY, NZ)
    stage_place = (dp, y, me, y, dp)

    def grad_start(stage):
        here, size = stage_place[stage], stage_size[stage]

        @pl.loop(1, size)
        def _(i):
            grad_copy(stage, lax.rem(here + i, size), here).start()

    def grad_wait(stage):
        here, size = stage_place[stage], stage_size[stage]

        @pl.loop(1, size)
        def _(i):
            frm = lax.rem(here + size - i, size)
            grad_copy(stage, frm, frm).wait_recv()

        @pl.loop(1, size)
        def _(i):
            grad_copy(stage, lax.rem(here + i, size), here).wait_send()

    def grad_begin():
        lane = lax.broadcasted_iota(jnp.int32, (BS, CH), 1)
        line = lax.broadcasted_iota(jnp.int32, (SUB, CH), 0)
        both = [jnp.broadcast_to(gb_ref[:, pl.ds(r * CH, CH)], (SUB, CH)) for r in range(2)]
        sums = jnp.where(line == 0, both[0], jnp.where(line == 1, both[1], 0.0))
        for i in range(NZ):
            part = gacc[i, pl.ds(0, BS), :]
            for n in range(1, NBLK):
                part = jnp.where(lane >= n * BS, gacc[i, pl.ds(n * BS, BS), :], part)
            gz[i, pl.ds(0, BS), :] = part.astype(BF16)
            gz[i, pl.ds(BS, SUB), :] = sums.astype(BF16)
        gzr[dp] = gz[dp]
        grad_start(0)

    def grad_finish(before_exchange, after_exchange_starts):
        part = BS // NY
        grad_wait(0)
        total = gzr[0].astype(F32)
        for i in range(1, NZ):
            total += gzr[i].astype(F32)
        for i in range(NY):
            gy[i, pl.ds(0, part), :] = total[i * part : (i + 1) * part]
            gy[i, pl.ds(part, 8), :] = total[BS : BS + 8]
        gyr[y] = gy[y]
        grad_start(1)
        before_exchange()
        grad_wait(1)
        gd[...] = gyr[0] + gyr[1] + gyr[2] + gyr[3]
        gdr[me] = gd[...]
        grad_start(2)
        after_exchange_starts()
        grad_wait(2)
        total = gdr[0]
        for i in range(1, ND):
            total += gdr[i]
        gd[...] = total
        gbout_ref[...] = gd[pl.ds(part, 8), lanes]
        gyo[y] = gd[pl.ds(0, part), lanes]
        grad_start(3)
        grad_wait(3)
        gzs[...] = gyo[...].reshape(BS, LANES).astype(BF16)
        gzo[dp] = gzs[...]
        grad_start(4)
        grad_wait(4)
        gout_ref[...] = gzo[...].astype(F32).reshape(NZ, NY, part, LANES)

    weights_start()
    load_table(0).wait()
    for g in range(NG):
        load(0, g).wait()
        lon_group(0, 0, g)
        x_start(15 + g)
    for i in range(1, 3):
        load_table(i).start()
    for j in range(1, NJ):
        lon_chunk(0, j)
        x_start(j)
    for g in range(NG):
        load(1, g).start()
    gacc[...] = jnp.zeros_like(gacc)
    gb_ref[...] = jnp.zeros_like(gb_ref)
    weights_build()
    for g in range(NG):
        load(1, g).wait()
    lon_chunk(1, 0)
    x_to_y(0, 0)
    for j in range(1, NJ):
        lon_chunk(1, j)
    x_to_y(0, 1)
    for i in range(1, 3):
        load_table(i).wait()
    for j in range(2):
        y_wait_recv(j)
        forward(j)
    x_to_y(0, 2)
    y_wait_recv(2)
    forward(2)
    x_to_y(1, 0)
    y_wait_recv(3)
    backward(0)
    back(0)
    x_to_y(1, 1)
    weight_grads(0)
    y_wait_recv(4)
    y_start(6)
    backward(1)
    back(1)
    y_wait_recv(6)
    x_start(6)
    x_to_y(1, 2)
    x_start(7)
    x_start(8)
    weight_grads(1)
    y_wait_recv(5)
    y_start(7)
    backward(2)
    weight_grads(2)
    grad_begin()
    back(2)
    y_wait_recv(7)
    x_start(9)
    x_start(10)
    y_start(8)

    def last_return():
        y_wait_recv(8)
        for g in range(NG):
            x_start(12 + g)

    grad_finish(lambda: x_start(11), last_return)
    for slot in range(6, 15):
        x_wait_recv(slot)
    for slot in range(1, 18):
        x_wait_send(slot)
    for slot in range(9):
        y_wait_send(slot)


def spectral_call(fields, cotangent, tw, th, tht, w_first, w_second, bias):
    vm = pl.BlockSpec(memory_space=pltpu.VMEM)
    hbm = pl.BlockSpec(memory_space=pl.ANY)
    dma = pltpu.SemaphoreType.DMA
    return pl.pallas_call(
        spectral_kernel,
        out_shape=(
            jax.ShapeDtypeStruct((NG, NJ, ND, NY, SUB, CH), BF16),
            jax.ShapeDtypeStruct((NZ, NY, BS // NY, LANES), F32),
            jax.ShapeDtypeStruct((8, LANES), F32),
        ),
        in_specs=[hbm] * 5 + [vm] * 3,
        out_specs=(hbm, vm, vm),
        scratch_shapes=[
            pltpu.VMEM((2, 2, 2, 2, BS, BS), BF16),
            pltpu.VMEM((2, 2, 2, BS), F32),
            pltpu.VMEM((2 * CH, 2 * CH), BF16),
            pltpu.VMEM((2 * CH, 2 * CH), BF16),
            pltpu.VMEM((1, 2 * CH), F32),
            pltpu.VMEM((4, CH, CH), F32),
            pltpu.VMEM((1, 2 * CH), F32),
            pltpu.VMEM((NZ, BS + SUB, CH), BF16),
            pltpu.VMEM((NZ, BS + SUB, CH), BF16),
            pltpu.VMEM((NY, BS // NY + 8, CH), F32),
            pltpu.VMEM((NY, BS // NY + 8, CH), F32),
            pltpu.VMEM((BS // NY + 8, CH), F32),
            pltpu.VMEM((ND, BS // NY + 8, CH), F32),
            pltpu.VMEM((NY, BS // NY, LANES), F32),
            pltpu.VMEM((BS, LANES), BF16),
            pltpu.VMEM((NZ, BS, LANES), BF16),
            pltpu.VMEM((2 * KW, HALF), BF16),
            pltpu.VMEM((2 * NLAT, 2 * NLAT), BF16),
            pltpu.VMEM((2 * NLAT, 2 * NLAT), BF16),
            pltpu.VMEM((ROWS, HALF, CH), BF16),
            pltpu.VMEM((3, GH * WAVES, 128), F32),
            pltpu.VMEM((2, NJ, ND, NG, NY, SUB, CH), BF16),
            pltpu.VMEM((2, NJ, ND, NG, NY, SUB, CH), BF16),
            pltpu.VMEM((2, NJ, NY, QROWS, CH), BF16),
            pltpu.VMEM((2, NJ, NY, QROWS, CH), BF16),
            pltpu.VMEM((NJ, NY, QROWS, CH), BF16),
            pltpu.VMEM((NJ, NY, QROWS, CH), BF16),
            pltpu.VMEM((NJ, NLAT, 2 * CH), BF16),
            pltpu.VMEM((NJ, NLAT, 2 * CH), BF16),
            pltpu.VMEM((NLAT, 2 * CH), BF16),
            pltpu.VMEM((NLAT, 2 * CH), BF16),
            pltpu.VMEM((NJ, NLAT, 2 * CH), F32),
            pltpu.VMEM((NJ, NLAT, 2 * CH), F32),
            pltpu.VMEM((2 * NLAT, CH), BF16),
            dma((2, NG)),
            dma((3,)),
            dma((18,)),
            dma((18, ND)),
            dma((18, ND)),
            dma((9,)),
            dma((9, NY)),
            dma((9, NY)),
            dma((3,)),
            dma((3,)),
            dma((3,)),
            dma((5, ND)),
            dma((5, ND)),
        ],
        compiler_params=pltpu.CompilerParams(
            collective_id=0, has_side_effects=True, vmem_limit_bytes=62 << 20
        ),
        cost_estimate=pl.CostEstimate(flops=10**10, bytes_accessed=3 * 10**7, transcendentals=10**6),
        name="spectral",
    )(fields, cotangent, tw, th, tht, w_first, w_second, bias)


PAIR = 2
TILE_W = 128


def inverse_kernel(
    back_hbm,
    cot_hbm,
    twt_hbm,
    grad_ref,
    bias_ref,
    out_hbm,
    g1_ref,
    g2_ref,
    gb_ref,
    bs,
    back,
    buf,
    twt,
    back_sem,
    cot_sem,
    out_sem,
    twt_sem,
):
    xhi = lax.axis_index("lon")

    def load_back(g):
        return pltpu.make_async_copy(back_hbm.at[g], back.at[g], back_sem.at[g])

    def load_cot(g):
        rows = pl.ds(g * GH, GH)
        return pltpu.make_async_copy(cot_hbm.at[0, rows], buf.at[rows], cot_sem.at[g])

    def store(i):
        rows = pl.ds(i * PAIR, PAIR)
        return pltpu.make_async_copy(buf.at[rows], out_hbm.at[0, rows], out_sem.at[i])

    table = pltpu.make_async_copy(twt_hbm.at[xhi], twt, twt_sem.at[0])
    load_back(0).start()
    table.start()
    load_cot(0).start()

    scale = 1.0 / math.sqrt(SPEC_ROWS)
    row = lax.broadcasted_iota(jnp.int32, (LANES, BS), 0)
    col = lax.broadcasted_iota(jnp.int32, (LANES, BS), 1)
    for m in range(2):
        pick = (row == col + (xhi * 64 + m * BS)).astype(F32)

        def take(value):
            return scale * jnp.dot(
                value, pick, precision=lax.Precision.HIGHEST, preferred_element_type=F32
            )

        for r in range(2):
            g1_ref[m, r] = take(grad_ref[r].reshape(BS, LANES))
            g2_ref[m, r] = take(grad_ref[2 + r].reshape(BS, LANES))
        gb_ref[m] = take(bias_ref[...])[:2]
    table.wait()

    @pl.loop(0, NG)
    def _(g):
        load_back(g).wait()

        @pl.when(g + 1 < NG)
        def _():
            load_back(g + 1).start()
            load_cot(g + 1).start()

        @pl.loop(0, NJ * ND)
        def _(jd):
            j, d = jd // ND, lax.rem(jd, ND)
            for ky in range(NY):
                rows = pl.ds(pl.multiple_of(jd * NY * SUB + ky * SUB, SUB), SUB)
                for ct in range(3):
                    bs[ct, rows, :] = back[g, j, d, ky, :, pl.ds(ct * 128, 128)].astype(F32)

        load_cot(g).wait()
        for hp in range(GH // PAIR):
            spec = jnp.concatenate(
                [
                    bs[ct, pl.ds(hp * PAIR + k, 2 * KW, stride=GH), :].astype(BF16)
                    for k in range(PAIR)
                    for ct in range(3)
                ],
                1,
            )
            for t in range(HALF // TILE_W):
                cols = pl.ds(t * TILE_W, TILE_W)
                part = dot(twt[cols, :], spec) * LON_NORM
                for k in range(PAIR):
                    h = g * GH + hp * PAIR + k
                    value = buf[h, cols].astype(F32) + part[:, k * CH : (k + 1) * CH]
                    buf[h, cols] = value.astype(BF16)
            store(g * (GH // PAIR) + hp).start()

    for i in range(ROWS // PAIR):
        store(i).wait()


def inverse_call(back, cotangent, twt, grads, bias):
    vm = pl.BlockSpec(memory_space=pltpu.VMEM)
    hbm = pl.BlockSpec(memory_space=pl.ANY)
    dma = pltpu.SemaphoreType.DMA
    return pl.pallas_call(
        inverse_kernel,
        out_shape=(
            jax.ShapeDtypeStruct((1, ROWS, HALF, CH), BF16),
            jax.ShapeDtypeStruct((2, 2, BS, BS), F32),
            jax.ShapeDtypeStruct((2, 2, BS, BS), F32),
            jax.ShapeDtypeStruct((2, 2, BS), F32),
        ),
        in_specs=[hbm, hbm, hbm, vm, vm],
        out_specs=(hbm, vm, vm, vm),
        scratch_shapes=[
            pltpu.VMEM((3, GH * 2 * KW, 128), F32),
            pltpu.VMEM((NG, NJ, ND, NY, SUB, CH), BF16),
            pltpu.VMEM((ROWS, HALF, CH), BF16),
            pltpu.VMEM((HALF, 2 * KW), BF16),
            dma((NG,)),
            dma((NG,)),
            dma((ROWS // PAIR,)),
            dma((1,)),
        ],
        compiler_params=pltpu.CompilerParams(vmem_limit_bytes=62 << 20),
        cost_estimate=pl.CostEstimate(
            flops=1400 * 10**6, bytes_accessed=18 * 10**6, transcendentals=0
        ),
        name="inverse",
    )(back, cotangent, twt, grads, bias)


def on_device(fields, cotangent, w_first, w_second, bias_first):
    tw, twt, th, tht = (jnp.asarray(table) for table in tables())
    back, grads, bias = spectral_call(
        fields, cotangent, tw, th, tht, w_first, w_second, bias_first
    )
    return inverse_call(back, cotangent, twt, grads, bias)


def solution(mesh):
    placed = (
        P("dp", "lat", "lon", None),
        P("dp", "lat", "lon", None),
        P("lon", None, None, None),
        P("lon", None, None, None),
        P("lon", None, None),
    )
    return jax.shard_map(
        on_device,
        mesh=mesh,
        in_specs=placed,
        out_specs=(
            P("dp", "lat", "lon", None),
            P("lon", None, None, None),
            P("lon", None, None, None),
            P("lon", None, None),
        ),
        check_vma=False,
    )
```
